32 devices in a mesh: bank: 2 (over x), gal: 16 (over z, y, core).
Axes of the slice: x: 2, y: 2, z: 4, core: 2. Of those that a mesh axis runs over, the one named last changes fastest.
Arguments:
- bank_queries: bfloat16 [256, 768], P(('bank', 'gal'))
- gallery: bfloat16 [65536, 768], P('gal')
- test_queries: bfloat16 [128, 768], P(('bank', 'gal'))
- test_slabs: int32 [128, 8], P('bank'), may hold values from 0 to 15, all different within a row; in each aligned block of 4 rows (0 to 3, 4 to 7, ...) at most 2 rows name the same one
- test_offsets: int32 [128, 8], P('bank'), may hold values from 0 to 31
Outputs:
- pooled: float32 [128, 768], P(('bank', 'gal'))
The draws below stay inside these ranges and needn't reach their ends.
Inputs may be any that keep to these rules, and one draw needn't show every extreme that they name: `test_slabs`: each row names 8 different slabs; the 4 rows of one device name no slab more than 2 times, and on some devices one slab exactly 2 times.
All inputs are finite; a program needn't handle non-finite values.
Results may differ from the reference program's by a relative error of at most 0.0065.
Values may be sent and summed in bfloat16 or wider, within the bound.
No kernel may reach another device: no remote copies, remote signals or barrier semaphores. Data moves between devices by JAX's collectives and lax.ppermute only.
A program may use at most 64 MiB of HBM per device.

```python
import math
import jax
import jax.numpy as jnp
import numpy as np
from jax import lax

D = 768
BLOCK = 128
NLIST = 8
ROUTE_CAP = 2
GAL_DEV = 4096
TQ_DEV = 4
NGAL = 65536
BANKQ = 256
TQUERIES = 128
N_GAL = 16


centre_count = 256


copy_noise = 0.3


def embed_rows(shared_key, row_key, positions):
    centres = jax.random.normal(jax.random.fold_in(shared_key, 3), (centre_count, D), jnp.float32)
    direction = jax.random.normal(jax.random.fold_in(shared_key, 5), (D,), jnp.float32)

    def one_row(position):
        pieces = jax.random.split(jax.random.fold_in(row_key, position), 4)
        alignment = jax.random.uniform(pieces[0], (), jnp.float32, -1.0, 1.0)
        loading = jax.random.uniform(pieces[1], (), jnp.float32, 0.2, 1.2)
        cluster = jax.random.randint(pieces[2], (), 0, centre_count)
        noise_part = jax.random.normal(pieces[3], (D,), jnp.float32)
        spread = jnp.float32(1.0)
        base_row = alignment * direction + loading * centres[cluster] + 0.8 * noise_part
        return (base_row, spread)
    return jax.vmap(one_row)(positions)


def draw_gallery(key, part):
    base_rows, spread = embed_rows(jax.random.fold_in(key, 101), jax.random.fold_in(key, 111), jnp.arange(NGAL, dtype=jnp.int32))
    return (base_rows * spread[:, None]).astype(jnp.bfloat16)


def draw_bank_queries(key, part):
    shared_key = jax.random.fold_in(key, 101)
    targets = jax.random.randint(jax.random.fold_in(key, 211), (BANKQ,), 0, NGAL)
    copied = jax.random.randint(jax.random.fold_in(key, 212), (BANKQ, 1), 0, 2).astype(jnp.float32)
    hub_rows, unused = embed_rows(shared_key, jax.random.fold_in(key, 111), targets)
    fresh_rows, spread = embed_rows(shared_key, jax.random.fold_in(key, 222), jnp.arange(BANKQ, dtype=jnp.int32))
    noise_part = jax.random.normal(jax.random.fold_in(key, 223), (BANKQ, D), jnp.float32)
    near_rows = hub_rows + copy_noise * noise_part
    mixed = copied * near_rows + (1.0 - copied) * fresh_rows
    return (mixed * spread[:, None]).astype(jnp.bfloat16)


def draw_test_queries(key, part):
    base_rows, spread = embed_rows(jax.random.fold_in(key, 101), jax.random.fold_in(key, 333), jnp.arange(TQUERIES, dtype=jnp.int32))
    return (base_rows * spread[:, None]).astype(jnp.bfloat16)


def place_ends(values, stream_key, smallest, largest):
    index_at = [jax.random.randint(jax.random.fold_in(stream_key, axis), (), 0, length) for axis, length in enumerate(values.shape)]
    main_axis = values.shape.index(max(values.shape))
    next_to = index_at[:main_axis] + [(index_at[main_axis] + 1) % values.shape[main_axis]] + index_at[main_axis + 1:]
    return values.at[tuple(index_at)].set(smallest).at[tuple(next_to)].set(largest)


def deal_out(rng, own, number, rows, amount, top, bound, slope):
    order = jax.random.permutation(rng, amount)
    packed, common = portions_of(amount, rows * top, bound, slope, True), portions_of(amount, rows * top, bound, slope, False)
    places = jnp.arange(amount)

    def named(tallies, rotation):
        used = int((tallies > 0).sum())
        fixed = max(1, used // 4)
        passed = fixed + (places - fixed + rotation * (used - fixed)) % max(1, amount - fixed)
        return jnp.zeros((amount,), jnp.int32).at[order[jnp.where(places < fixed, places, passed)]].set(jnp.asarray(tallies, jnp.int32))

    tallies = jnp.where(number % 4 == 0, named(packed, number // 4), named(common, number - number // 4 - 1))
    mixed = jax.random.permutation(jax.random.fold_in(own, 3), amount)
    donor, taker = mixed[0:amount // 2 * 2:2], mixed[1:amount // 2 * 2:2]
    room = jnp.minimum(tallies[donor] - 1, bound - tallies[taker]) // 2
    room = jnp.where((donor == order[0]) | (taker == order[0]) | (tallies[taker] == 0), 0, jnp.maximum(room, 0))
    passed = jax.random.randint(jax.random.fold_in(own, 4), (amount // 2,), 0, 1 << 20) % (room + 1)
    tallies = tallies.at[donor].add(-passed).at[taker].add(passed)
    members = jnp.searchsorted(jnp.cumsum(tallies), jnp.arange(rows * top), side="right").astype(jnp.int32)
    grid = members.reshape(top, rows).T
    grid = grid[jax.random.permutation(jax.random.fold_in(own, 1), rows)]
    rotation = jax.random.randint(jax.random.fold_in(own, 2), (rows, 1), 0, top)
    return jnp.take_along_axis(grid, (jnp.arange(top)[None, :] + rotation) % top, axis=1)


def portions_of(amount, total, reach, lean, full):
    weights = [(1 << 20) // math.isqrt(standing ** lean) + 1 for standing in range(1, amount + 1)]
    largest = reach if full else min(reach, max(-(-total // amount), total * weights[0] // sum(weights)))
    least = 1 if total - largest >= amount - 1 else 0
    holding, surplus = [largest] + [least] * (amount - 1), total - largest - least * (amount - 1)
    while surplus > 0:
        movable = [i for i in range(1, amount) if holding[i] < largest] or [i for i in range(1, amount) if holding[i] < reach]
        whole, left = sum([weights[i] for i in movable]), surplus
        for i in movable:
            extra = min(reach - holding[i], max(1, left * weights[i] // whole), surplus)
            holding[i] = holding[i] + extra
            surplus = surplus - extra
    return np.array(holding)


def setup_inputs(seed: int = 0) -> dict:
    seeds = jax.random.split(jax.random.key(seed), 6)
    bank_queries = draw_bank_queries(jax.random.fold_in(seeds[5], 71), 0)
    gallery = draw_gallery(jax.random.fold_in(seeds[5], 71), 0)
    test_queries = draw_test_queries(jax.random.fold_in(seeds[5], 71), 0)
    test_slabs_keys = jax.random.split(jax.random.fold_in(seeds[3], 1), TQUERIES // TQ_DEV)
    test_slabs_turns = jax.random.permutation(jax.random.fold_in(seeds[3], 3), TQUERIES // TQ_DEV)
    test_slabs = jax.vmap(lambda own, number: deal_out(jax.random.fold_in(seeds[3], 2), own, number, TQ_DEV, N_GAL, NLIST, ROUTE_CAP, 2))(test_slabs_keys, test_slabs_turns).reshape((TQUERIES, NLIST))
    test_offsets = place_ends(jax.random.randint(seeds[4], (TQUERIES, NLIST), 0, GAL_DEV // BLOCK), jax.random.fold_in(seeds[4], 1), 0, (GAL_DEV // BLOCK) - 1).astype(jnp.int32)
    return dict(bank_queries=bank_queries, gallery=gallery, test_queries=test_queries, test_slabs=test_slabs, test_offsets=test_offsets)


SHARPNESS = 20.0
epsilon = 1e-06

def row_scale(matrix):
    values = matrix.astype(jnp.float32)
    return lax.rsqrt(lax.optimization_barrier(jnp.sum(values * values, axis=1)) + epsilon)

def reference(bank_queries, gallery, test_queries, test_slabs, test_offsets):
    gallery_scale = row_scale(gallery)
    bank_scale = row_scale(bank_queries)
    test_scale = row_scale(test_queries)
    slab_rows = gallery.reshape(N_GAL, GAL_DEV, D)
    slab_scale = gallery_scale.reshape(N_GAL, GAL_DEV)

    def column_slab(inputs):
        rows_here, scale_here = inputs
        products = jnp.dot(bank_queries, rows_here.T, preferred_element_type=jnp.float32)
        scores = SHARPNESS * products * bank_scale[:, None] * scale_here[None, :]
        return lax.optimization_barrier(jnp.sum(jnp.exp(scores), axis=0))
    colsum = lax.map(column_slab, (slab_rows, slab_scale))
    log_col = jnp.log(colsum)
    blocks_here = GAL_DEV // BLOCK

    def test_slab(running_sums, inputs):
        numerator, denominator = running_sums
        rows_here, scale_here, logc_here, slab_index = inputs
        local_blocks = jnp.arange(blocks_here, dtype=jnp.int32)
        block_hits = (test_slabs == slab_index)[:, :, None] & (test_offsets[:, :, None] == local_blocks[None, None, :])
        listed = jnp.any(block_hits, axis=1)
        row_mask = jnp.repeat(listed, BLOCK, axis=1)
        products = jnp.dot(test_queries, rows_here.T, preferred_element_type=jnp.float32)
        logits = SHARPNESS * products * test_scale[:, None] * scale_here[None, :] - logc_here[None, :]
        weights = jnp.where(row_mask, jnp.exp(logits), jnp.float32(0.0))
        denominator = denominator + lax.optimization_barrier(jnp.sum(weights, axis=1))
        numerator = numerator + jnp.dot(weights.astype(jnp.bfloat16), rows_here, preferred_element_type=jnp.float32)
        return ((numerator, denominator), None)
    start_sums = (jnp.zeros((TQUERIES, D), jnp.float32), jnp.zeros((TQUERIES,), jnp.float32))
    (numerator, denominator), unused = lax.scan(test_slab, start_sums, (slab_rows, slab_scale, log_col, jnp.arange(N_GAL, dtype=jnp.int32)))
    return numerator / denominator[:, None]
```

```python
import functools

import jax
import jax.numpy as jnp
import numpy as np
from jax import lax
from jax.experimental import pallas as pl
from jax.experimental.pallas import tpu as pltpu
from jax.sharding import PartitionSpec as P

BLOCK = 128
CHUNKS = 8
LANES = 128
SHARPNESS = 20.0
LOG2E = 1.4426950408889634
epsilon = 1e-06

VMEM = pl.BlockSpec(memory_space=pltpu.VMEM)
SMEM = pl.BlockSpec(memory_space=pltpu.SMEM)
PARAMS = pltpu.CompilerParams(vmem_limit_bytes=24 << 20)


def keep(value):
    return pltpu.with_memory_space_constraint(value, pltpu.VMEM)


def load_kernel(gallery_hbm, gallery_ref, scale_ref, sems):
    rows, depth = gallery_hbm.shape
    part = rows // CHUNKS
    copies = [
        pltpu.make_async_copy(
            gallery_hbm.at[pl.ds(c * part, part)], gallery_ref.at[pl.ds(c * part, part)], sems.at[c]
        )
        for c in range(CHUNKS)
    ]
    for copy in copies:
        copy.start()
    for c in range(CHUNKS):
        copies[c].wait()
        values = gallery_ref[pl.ds(c * part, part), :].astype(jnp.float32)
        squares = values * values
        folded = squares[:, :LANES]
        for k in range(1, depth // LANES):
            folded = folded + squares[:, k * LANES : (k + 1) * LANES]
        for b in range(part // BLOCK):
            total = jnp.sum(folded[b * BLOCK : (b + 1) * BLOCK].T, axis=0, keepdims=True)
            scale_ref[c : c + 1, b * BLOCK : (b + 1) * BLOCK] = lax.rsqrt(total + epsilon)


def load(gallery):
    rows, _ = gallery.shape
    return pl.pallas_call(
        load_kernel,
        out_shape=(
            pltpu.VMEM(gallery.shape, gallery.dtype),
            pltpu.VMEM((CHUNKS, rows // CHUNKS), jnp.float32),
        ),
        in_specs=[pl.BlockSpec(memory_space=pl.ANY)],
        out_specs=(VMEM, VMEM),
        scratch_shapes=[pltpu.SemaphoreType.DMA((CHUNKS,))],
        compiler_params=PARAMS,
        name="load",
    )(gallery)


def score_kernel(bank_rows, query_ref, gallery_ref, scale_ref, block_ref, colsum_ref, listed_ref):
    queries = query_ref[...]
    wide = queries.astype(jnp.float32)
    query_scale = lax.rsqrt(jnp.sum(wide * wide, axis=1, keepdims=True) + epsilon) * (SHARPNESS * LOG2E)
    test_rows = queries.shape[0] - bank_rows
    part = gallery_ref.shape[0] // CHUNKS
    block = block_ref[...]
    picked = jnp.zeros((test_rows, BLOCK), jnp.float32)
    for c in range(CHUNKS):
        scores = lax.dot_general(
            queries,
            gallery_ref[pl.ds(c * part, part), :],
            (((1,), (1,)), ((), ())),
            preferred_element_type=jnp.float32,
        )
        scores = scores * scale_ref[c : c + 1, :]
        exps = jnp.exp2(scores[:bank_rows] * query_scale[:bank_rows])
        colsum_ref[c : c + 1, :] = jnp.sum(exps, axis=0, keepdims=True)
        for b in range(part // BLOCK):
            here = scores[bank_rows:, b * BLOCK : (b + 1) * BLOCK]
            picked = jnp.where(block == c * (part // BLOCK) + b, here, picked)
    listed_ref[...] = jnp.exp2(picked * query_scale[bank_rows:])


def score(queries, gallery, scale, block, bank_rows):
    test_rows = queries.shape[0] - bank_rows
    return pl.pallas_call(
        functools.partial(score_kernel, bank_rows),
        out_shape=(pltpu.VMEM(scale.shape, jnp.float32), pltpu.VMEM((test_rows, BLOCK), jnp.float32)),
        in_specs=[VMEM] * 4,
        out_specs=(VMEM, VMEM),
        compiler_params=PARAMS,
        name="score",
    )(queries, keep(gallery), keep(scale), block)


def pool_kernel(order, me_ref, listed_ref, own_ref, other_ref, gallery_ref, block_ref, out_ref, weight_ref):
    block = block_ref[...]
    test_rows = block.shape[0]
    rows, depth = gallery_ref.shape
    each = rows // BLOCK // CHUNKS
    inverse = 1.0 / (own_ref[...] + other_ref[...])
    picked = jnp.zeros((test_rows, BLOCK), jnp.float32)
    for b in range(rows // BLOCK):
        c, at = b // each, (b % each) * BLOCK
        picked = jnp.where(block == b, inverse[c : c + 1, at : at + BLOCK], picked)
    weight = listed_ref[...] * picked
    total = jnp.sum(weight, axis=1, keepdims=True)
    for b in range(rows // BLOCK):
        weight_ref[:, b * BLOCK : (b + 1) * BLOCK] = jnp.where(block == b, weight, 0.0).astype(jnp.bfloat16)
    numerator = jnp.dot(weight_ref[...], gallery_ref[...], preferred_element_type=jnp.float32)
    high = total.astype(jnp.bfloat16).astype(jnp.float32)
    lane = lax.broadcasted_iota(jnp.int32, (test_rows, LANES), 1)
    tail = jnp.where(lane == 0, high, jnp.where(lane == 1, total - high, 0.0))
    own = test_rows // len(order)
    for i, bits in enumerate(order):
        to = me_ref[0] ^ bits
        out_ref[to, :, :depth] = numerator[i * own : (i + 1) * own].astype(jnp.bfloat16)
        out_ref[to, :, depth:] = tail[i * own : (i + 1) * own].astype(jnp.bfloat16)


def pool(order, me, listed, own, other, gallery, block):
    rows, depth = gallery.shape
    test_rows = listed.shape[0]
    return pl.pallas_call(
        functools.partial(pool_kernel, order),
        out_shape=pltpu.VMEM((len(order), test_rows // len(order), depth + LANES), jnp.bfloat16),
        in_specs=[SMEM] + [VMEM] * 5,
        out_specs=VMEM,
        scratch_shapes=[pltpu.VMEM((test_rows, rows), jnp.bfloat16)],
        compiler_params=PARAMS,
        name="pool",
    )(me, keep(listed), keep(own), other, keep(gallery), block)


def swap(value, axis, size, bit):
    return lax.ppermute(value, axis, [(i, i ^ bit) for i in range(size)])


def body(devices, banks, bank_queries, gallery, test_queries, test_slabs, test_offsets):
    me = lax.axis_index("gal")
    bank_own, test_own = bank_queries.shape[0], test_queries.shape[0]

    order = [0]
    bank, test = bank_queries, test_queries
    bit = devices // 2
    while bit:
        packed = jnp.concatenate([bank, test], axis=0)
        other = swap(packed, "gal", devices, bit)
        bank = jnp.concatenate([bank, other[: bank.shape[0]]], axis=0)
        test = jnp.concatenate([test, other[-test.shape[0] :]], axis=0)
        order = order + [o ^ bit for o in order]
        bit //= 2
    queries = jnp.concatenate([bank, test], axis=0)

    place = (me ^ np.array(order, np.int32))[:, None] * test_own + np.arange(test_own, dtype=np.int32)[None, :]
    found = jnp.sum(jnp.where(test_slabs == me, test_offsets + 1, 0), axis=1) - 1
    group = np.arange(devices * test_own, dtype=np.int32)
    block = jnp.sum(jnp.where(place.reshape(-1, 1) == group[None, :], found[None, :], 0), axis=1)
    block = jnp.broadcast_to(block[:, None], (devices * test_own, LANES))

    gallery, scale = load(gallery)
    colsum, listed = score(queries, gallery, scale, block, devices * bank_own)
    bit = banks // 2
    other = jnp.zeros_like(colsum)
    while bit:
        other = swap(colsum, "bank", banks, bit)
        bit //= 2
        if bit:
            colsum = colsum + other
    sums = pool(order, me.reshape(1), listed, colsum, other, gallery, block)
    sums = lax.all_to_all(sums, "gal", 0, 0, tiled=True)
    sums = jnp.sum(sums.astype(jnp.float32), axis=0)
    depth = gallery.shape[1]
    return sums[:, :depth] / (sums[:, depth] + sums[:, depth + 1])[:, None]


def solution(mesh):
    in_specs = (
        P(("bank", "gal"), None),
        P("gal", None),
        P(("bank", "gal"), None),
        P("bank", None),
        P("bank", None),
    )
    out_specs = P(("bank", "gal"), None)
    local = functools.partial(body, mesh.shape["gal"], mesh.shape["bank"])
    return jax.shard_map(local, mesh=mesh, in_specs=in_specs, out_specs=out_specs, check_vma=False)
```

```python
import functools

import jax
import jax.numpy as jnp
from jax import lax
from jax.experimental import pallas as pl
from jax.experimental.pallas import tpu as pltpu
from jax.sharding import PartitionSpec as P

BLOCK = 128
CHUNKS = 8
LANES = 128
CAP = 2
SHARPNESS = 20.0
LOG2E = 1.4426950408889634
epsilon = 1e-06

VMEM = pl.BlockSpec(memory_space=pltpu.VMEM)
HBM = pl.BlockSpec(memory_space=pltpu.HBM)
PARAMS = pltpu.CompilerParams(vmem_limit_bytes=16 << 20)


def in_hbm(value):
    return pltpu.with_memory_space_constraint(value, pltpu.HBM)


def keep(value):
    return pltpu.with_memory_space_constraint(value, pltpu.VMEM)


def pack_kernel(bank_hbm, test_hbm, packed_ref, bank_ref, test_ref, sems):
    copies = [
        pltpu.make_async_copy(bank_hbm, bank_ref, sems.at[0]),
        pltpu.make_async_copy(test_hbm, test_ref, sems.at[1]),
    ]
    for copy in copies:
        copy.start()
    for copy in copies:
        copy.wait()
    rows = bank_ref.shape[0]
    packed_ref[:rows, :] = bank_ref[...]
    packed_ref[rows:, :] = test_ref[...]


def pack(bank, test):
    return pl.pallas_call(
        pack_kernel,
        out_shape=pltpu.VMEM((bank.shape[0] + test.shape[0], bank.shape[1]), bank.dtype),
        in_specs=[HBM, HBM],
        out_specs=VMEM,
        scratch_shapes=[
            pltpu.VMEM(bank.shape, bank.dtype),
            pltpu.VMEM(test.shape, test.dtype),
            pltpu.SemaphoreType.DMA((2,)),
        ],
        compiler_params=PARAMS,
        name="pack",
    )(in_hbm(bank), in_hbm(test))


def bits_of(index, masks):
    value = jnp.zeros_like(index)
    for k, mask in enumerate(masks):
        value = value ^ jnp.where((index >> k) & 1 == 1, mask, 0)
    return value


def iota(shape, axis):
    return lax.broadcasted_iota(jnp.int32, shape, axis)


def route(masks, bank_own, test_own, slabs, offsets, pick_ref, block_ref, spread_ref):
    me = lax.axis_index("gal")
    devices = 1 << len(masks)
    group = devices * test_own
    own = bank_own + test_own
    bank_rows = devices * bank_own
    slots = devices * CAP

    found = jnp.sum(jnp.where(slabs == me, offsets + 1, 0), axis=0, keepdims=True)
    before = (iota((group, group), 0) // test_own == iota((group, group), 1) // test_own) & (
        iota((group, group), 0) < iota((group, group), 1)
    )
    flags = jnp.broadcast_to(jnp.where(found > 0, 1.0, 0.0), (8, group)).astype(jnp.bfloat16)
    rank = jnp.dot(flags, jnp.where(before, 1.0, 0.0).astype(jnp.bfloat16), preferred_element_type=jnp.float32)
    rank = rank[:1].astype(jnp.int32)
    index = iota((slots, group), 0)
    column = iota((slots, group), 1)
    filled = (column // test_own == me ^ bits_of(index // CAP, masks)) & (found > 0) & (rank == index % CAP)
    block = jnp.sum(jnp.where(filled, found, 0), axis=1, keepdims=True) - 1
    block_ref[...] = jnp.broadcast_to(block, block_ref.shape)
    from_row = jnp.sum(jnp.where(filled, column % test_own + 1, 0), axis=1, keepdims=True)
    index = iota((slots, 1), 0) // CAP
    slot_from = jnp.where(from_row > 0, index * own + bank_own - 1 + from_row, -1)
    index = iota((bank_rows, 1), 0)
    bank_from = index // bank_own * own + index % bank_own
    half = pick_ref.shape[2]
    for h in range(2):
        column = iota((bank_rows, half), 1) + h * half
        pick_ref[h, :bank_rows, :] = jnp.where(column == bank_from, 1.0, 0.0).astype(jnp.bfloat16)
        column = iota((slots, half), 1) + h * half
        pick_ref[h, bank_rows:, :] = jnp.where(column == slot_from, 1.0, 0.0).astype(jnp.bfloat16)

    lane = iota((1, slots), 1)
    filled_before = jnp.zeros((1, slots), jnp.int32)
    mine = iota(slabs.shape, 1)
    for r in range(test_own):
        listed = jnp.sum(jnp.where(mine == me * test_own + r, slabs, 0), axis=1, keepdims=True)
        here = jnp.sum(jnp.where(listed == lane // CAP, 1, 0), axis=0, keepdims=True)
        spread_ref[r : r + 1, :] = jnp.where((here > 0) & (filled_before == lane % CAP), 1.0, 0.0)
        filled_before = filled_before + here


def load_kernel(
    masks, bank_own, test_own, gallery_hbm, packed_ref, slabs_hbm, offsets_hbm,
    gallery_ref, scale_ref, packed_out, pick_ref, block_ref, spread_ref, slabs_ref, offsets_ref, sems, small_sems,
):
    rows, depth = gallery_hbm.shape
    part = rows // CHUNKS
    small = [
        pltpu.make_async_copy(slabs_hbm, slabs_ref, small_sems.at[0]),
        pltpu.make_async_copy(offsets_hbm, offsets_ref, small_sems.at[1]),
    ]
    copies = [
        pltpu.make_async_copy(
            gallery_hbm.at[pl.ds(c * part, part)], gallery_ref.at[pl.ds(c * part, part)], sems.at[c]
        )
        for c in range(CHUNKS)
    ]
    for copy in small + copies:
        copy.start()
    packed_out[...] = packed_ref[...]
    for copy in small:
        copy.wait()
    route(masks, bank_own, test_own, slabs_ref[...], offsets_ref[...], pick_ref, block_ref, spread_ref)
    for c in range(CHUNKS):
        copies[c].wait()
        values = gallery_ref[pl.ds(c * part, part), :].astype(jnp.float32)
        squares = values * values
        folded = squares[:, :LANES]
        for k in range(1, depth // LANES):
            folded = folded + squares[:, k * LANES : (k + 1) * LANES]
        for b in range(part // BLOCK):
            total = jnp.sum(folded[b * BLOCK : (b + 1) * BLOCK].T, axis=0, keepdims=True)
            scale_ref[c : c + 1, b * BLOCK : (b + 1) * BLOCK] = lax.rsqrt(total + epsilon)


def load(masks, bank_own, test_own, gallery, packed, slabs, offsets):
    rows, depth = gallery.shape
    devices = 1 << len(masks)
    slots = devices * CAP
    half = devices * (bank_own + test_own) // 2
    return pl.pallas_call(
        functools.partial(load_kernel, masks, bank_own, test_own),
        out_shape=(
            pltpu.VMEM(gallery.shape, gallery.dtype),
            pltpu.VMEM((CHUNKS, rows // CHUNKS), jnp.float32),
            pltpu.VMEM(packed.shape, packed.dtype),
            pltpu.VMEM((2, devices * bank_own + slots, half), jnp.bfloat16),
            pltpu.VMEM((slots, LANES), jnp.int32),
            pltpu.VMEM((test_own, slots), jnp.float32),
        ),
        in_specs=[HBM, VMEM, HBM, HBM],
        out_specs=(VMEM,) * 6,
        scratch_shapes=[
            pltpu.VMEM(slabs.shape, slabs.dtype),
            pltpu.VMEM(offsets.shape, offsets.dtype),
            pltpu.SemaphoreType.DMA((CHUNKS,)),
            pltpu.SemaphoreType.DMA((2,)),
        ],
        compiler_params=PARAMS,
        name="load",
    )(in_hbm(gallery), packed, in_hbm(slabs), in_hbm(offsets))


def score_kernel(first_ref, second_ref, pick_ref, gallery_ref, scale_ref, block_ref, colsum_ref, listed_ref):
    wide = jnp.dot(pick_ref[0], first_ref[...], preferred_element_type=jnp.float32)
    wide = wide + jnp.dot(pick_ref[1], second_ref[...], preferred_element_type=jnp.float32)
    queries = wide.astype(jnp.bfloat16)
    query_scale = lax.rsqrt(jnp.sum(wide * wide, axis=1, keepdims=True) + epsilon) * (SHARPNESS * LOG2E)
    slots = block_ref.shape[0]
    bank_rows = queries.shape[0] - slots
    part = scale_ref.shape[1]
    block = block_ref[...]
    picked = jnp.zeros((slots, BLOCK), jnp.float32)
    for c in range(CHUNKS):
        scores = lax.dot_general(
            queries,
            gallery_ref[pl.ds(c * part, part), :],
            (((1,), (1,)), ((), ())),
            preferred_element_type=jnp.float32,
        )
        scores = scores * scale_ref[c : c + 1, :]
        exps = jnp.exp2(scores[:bank_rows] * query_scale[:bank_rows])
        colsum_ref[c : c + 1, :] = jnp.sum(exps, axis=0, keepdims=True)
        for b in range(part // BLOCK):
            here = scores[bank_rows:, b * BLOCK : (b + 1) * BLOCK]
            picked = jnp.where(block == c * (part // BLOCK) + b, here, picked)
    listed_ref[...] = jnp.exp2(picked * query_scale[bank_rows:])


def score(first, second, pick, gallery, scale, block):
    return pl.pallas_call(
        score_kernel,
        out_shape=(pltpu.VMEM(scale.shape, jnp.float32), pltpu.VMEM((block.shape[0], BLOCK), jnp.float32)),
        in_specs=[VMEM] * 6,
        out_specs=(VMEM, VMEM),
        compiler_params=PARAMS,
        name="score",
    )(keep(first), second, keep(pick), keep(gallery), keep(scale), keep(block))


def pool_kernel(order, listed_ref, own_ref, other_ref, gallery_ref, block_ref, out_ref, weight_ref):
    block = block_ref[...]
    slots = block.shape[0]
    rows, depth = gallery_ref.shape
    each = rows // BLOCK // CHUNKS
    inverse = 1.0 / (own_ref[...] + other_ref[...])
    picked = jnp.zeros((slots, BLOCK), jnp.float32)
    for b in range(rows // BLOCK):
        c, at = b // each, (b % each) * BLOCK
        picked = jnp.where(block == b, inverse[c : c + 1, at : at + BLOCK], picked)
    weight = listed_ref[...] * picked
    total = jnp.sum(weight, axis=1, keepdims=True)
    for b in range(rows // BLOCK):
        weight_ref[:, b * BLOCK : (b + 1) * BLOCK] = jnp.where(block == b, weight, 0.0).astype(jnp.bfloat16)
    numerator = jnp.dot(weight_ref[...], gallery_ref[...], preferred_element_type=jnp.float32)
    high = total.astype(jnp.bfloat16).astype(jnp.float32)
    lane = iota((slots, LANES), 1)
    tail = jnp.where(lane == 0, high, jnp.where(lane == 1, total - high, 0.0))
    me = lax.axis_index("gal")
    for i, bits in enumerate(order):
        at = slice(i * CAP, (i + 1) * CAP)
        out_ref[me ^ bits, :, :depth] = numerator[at].astype(jnp.bfloat16)
        out_ref[me ^ bits, :, depth:] = tail[at].astype(jnp.bfloat16)


def pool(order, listed, own, other, gallery, block):
    rows, depth = gallery.shape
    slots = listed.shape[0]
    return pl.pallas_call(
        functools.partial(pool_kernel, order),
        out_shape=pltpu.VMEM((len(order), CAP, depth + LANES), jnp.bfloat16),
        in_specs=[VMEM] * 5,
        out_specs=VMEM,
        scratch_shapes=[pltpu.VMEM((slots, rows), jnp.bfloat16)],
        compiler_params=PARAMS,
        name="pool",
    )(keep(listed), keep(own), other, keep(gallery), keep(block))


def finish_kernel(sums_ref, spread_ref, out_ref):
    depth = out_ref.shape[1]
    sums = jnp.concatenate([sums_ref[s].astype(jnp.float32) for s in range(sums_ref.shape[0])], axis=0)
    sums = jnp.dot(
        spread_ref[...].astype(jnp.bfloat16), sums.astype(jnp.bfloat16), preferred_element_type=jnp.float32
    )
    out_ref[...] = sums[:, :depth] / (sums[:, depth : depth + 1] + sums[:, depth + 1 : depth + 2])


def finish(sums, spread):
    return pl.pallas_call(
        finish_kernel,
        out_shape=jax.ShapeDtypeStruct((spread.shape[0], sums.shape[2] - LANES), jnp.float32),
        in_specs=[VMEM, VMEM],
        out_specs=VMEM,
        compiler_params=PARAMS,
        name="finish",
    )(sums, keep(spread))


def swap(value, axis, size, bit):
    return lax.ppermute(value, axis, [(i, i ^ bit) for i in range(size)])


def body(devices, banks, bank_queries, gallery, test_queries, test_slabs, test_offsets):
    bank_own, test_own = bank_queries.shape[0], test_queries.shape[0]

    masks = [devices >> (i + 1) | 1 for i in range(devices.bit_length() - 1)]
    order = [0]
    for mask in masks:
        order = order + [o ^ mask for o in order]

    packed = pack(bank_queries, test_queries)
    other = swap(packed, "gal", devices, masks[0])
    gallery, scale, packed, pick, block, spread = load(
        masks, bank_own, test_own, gallery, packed, test_slabs.T, test_offsets.T
    )
    for mask in masks[1:]:
        packed = jnp.concatenate([packed, other], axis=0)
        other = swap(packed, "gal", devices, mask)

    colsum, listed = score(packed, other, pick, gallery, scale, block)
    bit = banks // 2
    other = jnp.zeros_like(colsum)
    while bit:
        other = swap(colsum, "bank", banks, bit)
        bit //= 2
        if bit:
            colsum = colsum + other
    sums = pool(order, listed, colsum, other, gallery, block)
    sums = lax.all_to_all(sums, "gal", 0, 0, tiled=True)
    return finish(sums, spread)


def solution(mesh):
    in_specs = (
        P(("bank", "gal"), None),
        P("gal", None),
        P(("bank", "gal"), None),
        P("bank", None),
        P("bank", None),
    )
    out_specs = P(("bank", "gal"), None)
    local = functools.partial(body, mesh.shape["gal"], mesh.shape["bank"])
    return jax.shard_map(local, mesh=mesh, in_specs=in_specs, out_specs=out_specs, check_vma=False)
```

```python
import functools

import jax
import jax.numpy as jnp
from jax import lax
from jax.experimental import pallas as pl
from jax.experimental.pallas import tpu as pltpu
from jax.sharding import PartitionSpec as P

BLOCK = 128
CHUNKS = 8
LANES = 128
CAP = 2
SHARPNESS = 20.0
LOG2E = 1.4426950408889634
epsilon = 1e-06

VMEM = pl.BlockSpec(memory_space=pltpu.VMEM)
HBM = pl.BlockSpec(memory_space=pltpu.HBM)
PARAMS = pltpu.CompilerParams(vmem_limit_bytes=16 << 20)


def in_hbm(value):
    return pltpu.with_memory_space_constraint(value, pltpu.HBM)


def keep(value):
    return pltpu.with_memory_space_constraint(value, pltpu.VMEM)


def pack_kernel(bank_hbm, test_hbm, packed_ref, bank_ref, test_ref, sems):
    copies = [
        pltpu.make_async_copy(bank_hbm, bank_ref, sems.at[0]),
        pltpu.make_async_copy(test_hbm, test_ref, sems.at[1]),
    ]
    for copy in copies:
        copy.start()
    for copy in copies:
        copy.wait()
    rows = bank_ref.shape[0]
    packed_ref[:rows, :] = bank_ref[...]
    packed_ref[rows:, :] = test_ref[...]


def pack(bank, test):
    return pl.pallas_call(
        pack_kernel,
        out_shape=pltpu.VMEM((bank.shape[0] + test.shape[0], bank.shape[1]), bank.dtype),
        in_specs=[HBM, HBM],
        out_specs=VMEM,
        scratch_shapes=[
            pltpu.VMEM(bank.shape, bank.dtype),
            pltpu.VMEM(test.shape, test.dtype),
            pltpu.SemaphoreType.DMA((2,)),
        ],
        compiler_params=PARAMS,
        name="pack",
    )(in_hbm(bank), in_hbm(test))


def bits_of(index, masks):
    value = jnp.zeros_like(index)
    for k, mask in enumerate(masks):
        value = value ^ jnp.where((index >> k) & 1 == 1, mask, 0)
    return value


def iota(shape, axis):
    return lax.broadcasted_iota(jnp.int32, shape, axis)


def route(masks, bank_own, test_own, slabs, offsets, pick_ref, block_ref, spread_ref):
    me = lax.axis_index("gal")
    devices = 1 << len(masks)
    group = devices * test_own
    own = bank_own + test_own
    bank_rows = devices * bank_own
    slots = devices * CAP

    found = jnp.sum(jnp.where(slabs == me, offsets + 1, 0), axis=0, keepdims=True)
    before = (iota((group, group), 0) // test_own == iota((group, group), 1) // test_own) & (
        iota((group, group), 0) < iota((group, group), 1)
    )
    flags = jnp.broadcast_to(jnp.where(found > 0, 1.0, 0.0), (8, group)).astype(jnp.bfloat16)
    rank = jnp.dot(flags, jnp.where(before, 1.0, 0.0).astype(jnp.bfloat16), preferred_element_type=jnp.float32)
    rank = rank[:1].astype(jnp.int32)
    index = iota((slots, group), 0)
    column = iota((slots, group), 1)
    filled = (column // test_own == me ^ bits_of(index // CAP, masks)) & (found > 0) & (rank == index % CAP)
    block = jnp.sum(jnp.where(filled, found, 0), axis=1, keepdims=True) - 1
    block_ref[...] = jnp.broadcast_to(block, block_ref.shape)
    from_row = jnp.sum(jnp.where(filled, column % test_own + 1, 0), axis=1, keepdims=True)
    index = iota((slots, 1), 0) // CAP
    slot_from = jnp.where(from_row > 0, index * own + bank_own - 1 + from_row, -1)
    index = iota((bank_rows, 1), 0)
    bank_from = index // bank_own * own + index % bank_own
    half = pick_ref.shape[2]
    for h in range(2):
        column = iota((bank_rows, half), 1) + h * half
        pick_ref[h, :bank_rows, :] = jnp.where(column == bank_from, 1.0, 0.0).astype(jnp.bfloat16)
        column = iota((slots, half), 1) + h * half
        pick_ref[h, bank_rows:, :] = jnp.where(column == slot_from, 1.0, 0.0).astype(jnp.bfloat16)

    lane = iota((1, slots), 1)
    filled_before = jnp.zeros((1, slots), jnp.int32)
    mine = iota(slabs.shape, 1)
    for r in range(test_own):
        listed = jnp.sum(jnp.where(mine == me * test_own + r, slabs, 0), axis=1, keepdims=True)
        here = jnp.sum(jnp.where(listed == lane // CAP, 1, 0), axis=0, keepdims=True)
        spread_ref[r : r + 1, :] = jnp.where((here > 0) & (filled_before == lane % CAP), 1.0, 0.0)
        filled_before = filled_before + here


def load_kernel(
    masks, bank_own, test_own, gallery_hbm, packed_ref, slabs_hbm, offsets_hbm,
    gallery_ref, scale_ref, packed_out, pick_ref, block_ref, spread_ref, slabs_ref, offsets_ref, sems, small_sems,
):
    rows, depth = gallery_hbm.shape
    part = rows // CHUNKS
    small = [
        pltpu.make_async_copy(slabs_hbm, slabs_ref, small_sems.at[0]),
        pltpu.make_async_copy(offsets_hbm, offsets_ref, small_sems.at[1]),
    ]
    copies = [
        pltpu.make_async_copy(
            gallery_hbm.at[pl.ds(c * part, part)], gallery_ref.at[pl.ds(c * part, part)], sems.at[c]
        )
        for c in range(CHUNKS)
    ]
    for copy in small + copies:
        copy.start()
    packed_out[...] = packed_ref[...]
    for copy in small:
        copy.wait()
    route(masks, bank_own, test_own, slabs_ref[...], offsets_ref[...], pick_ref, block_ref, spread_ref)
    for c in range(CHUNKS):
        copies[c].wait()
        values = gallery_ref[pl.ds(c * part, part), :].astype(jnp.float32)
        squares = values * values
        folded = squares[:, :LANES]
        for k in range(1, depth // LANES):
            folded = folded + squares[:, k * LANES : (k + 1) * LANES]
        for b in range(part // BLOCK):
            total = jnp.sum(folded[b * BLOCK : (b + 1) * BLOCK].T, axis=0, keepdims=True)
            scale_ref[c : c + 1, b * BLOCK : (b + 1) * BLOCK] = lax.rsqrt(total + epsilon)


def load(masks, bank_own, test_own, gallery, packed, slabs, offsets):
    rows, depth = gallery.shape
    devices = 1 << len(masks)
    slots = devices * CAP
    half = devices * (bank_own + test_own) // 2
    return pl.pallas_call(
        functools.partial(load_kernel, masks, bank_own, test_own),
        out_shape=(
            pltpu.VMEM(gallery.shape, gallery.dtype),
            pltpu.VMEM((CHUNKS, rows // CHUNKS), jnp.float32),
            pltpu.VMEM(packed.shape, packed.dtype),
            pltpu.VMEM((2, devices * bank_own + slots, half), jnp.bfloat16),
            pltpu.VMEM((slots, LANES), jnp.int32),
            pltpu.VMEM((test_own, slots), jnp.float32),
        ),
        in_specs=[HBM, VMEM, HBM, HBM],
        out_specs=(VMEM,) * 6,
        scratch_shapes=[
            pltpu.VMEM(slabs.shape, slabs.dtype),
            pltpu.VMEM(offsets.shape, offsets.dtype),
            pltpu.SemaphoreType.DMA((CHUNKS,)),
            pltpu.SemaphoreType.DMA((2,)),
        ],
        compiler_params=PARAMS,
        name="load",
    )(in_hbm(gallery), packed, in_hbm(slabs), in_hbm(offsets))


def score_kernel(first_ref, second_ref, pick_ref, gallery_ref, scale_ref, block_ref, colsum_ref, listed_ref):
    wide = jnp.dot(pick_ref[0], first_ref[...], preferred_element_type=jnp.float32)
    wide = wide + jnp.dot(pick_ref[1], second_ref[...], preferred_element_type=jnp.float32)
    queries = wide.astype(jnp.bfloat16)
    query_scale = lax.rsqrt(jnp.sum(wide * wide, axis=1, keepdims=True) + epsilon) * (SHARPNESS * LOG2E)
    slots = block_ref.shape[0]
    bank_rows = queries.shape[0] - slots
    part = scale_ref.shape[1]
    block = block_ref[...]
    picked = jnp.zeros((slots, BLOCK), jnp.float32)
    for c in range(CHUNKS):
        scores = lax.dot_general(
            queries,
            gallery_ref[pl.ds(c * part, part), :],
            (((1,), (1,)), ((), ())),
            preferred_element_type=jnp.float32,
        )
        scores = scores * scale_ref[c : c + 1, :]
        exps = jnp.exp2(scores[:bank_rows] * query_scale[:bank_rows])
        colsum_ref[c : c + 1, :] = jnp.sum(exps, axis=0, keepdims=True)
        for b in range(part // BLOCK):
            here = scores[bank_rows:, b * BLOCK : (b + 1) * BLOCK]
            picked = jnp.where(block == c * (part // BLOCK) + b, here, picked)
    listed_ref[...] = jnp.exp2(picked * query_scale[bank_rows:])


def score(first, second, pick, gallery, scale, block):
    return pl.pallas_call(
        score_kernel,
        out_shape=(pltpu.VMEM(scale.shape, jnp.float32), pltpu.VMEM((block.shape[0], BLOCK), jnp.float32)),
        in_specs=[VMEM] * 6,
        out_specs=(VMEM, VMEM),
        compiler_params=PARAMS,
        name="score",
    )(keep(first), second, keep(pick), keep(gallery), keep(scale), keep(block))


def pool_kernel(order, listed_ref, own_ref, other_ref, gallery_ref, block_ref, out_ref, weight_ref):
    block = block_ref[...]
    slots = block.shape[0]
    rows, depth = gallery_ref.shape
    each = rows // BLOCK // CHUNKS
    inverse = 1.0 / (own_ref[...] + other_ref[...])
    picked = jnp.zeros((slots, BLOCK), jnp.float32)
    for b in range(rows // BLOCK):
        c, at = b // each, (b % each) * BLOCK
        picked = jnp.where(block == b, inverse[c : c + 1, at : at + BLOCK], picked)
    weight = listed_ref[...] * picked
    total = jnp.sum(weight, axis=1, keepdims=True)
    for b in range(rows // BLOCK):
        weight_ref[:, b * BLOCK : (b + 1) * BLOCK] = jnp.where(block == b, weight, 0.0).astype(jnp.bfloat16)
    numerator = jnp.dot(weight_ref[...], gallery_ref[...], preferred_element_type=jnp.float32)
    high = total.astype(jnp.bfloat16).astype(jnp.float32)
    lane = iota((slots, LANES), 1)
    tail = jnp.where(lane == 0, high, jnp.where(lane == 1, total - high, 0.0))
    me = lax.axis_index("gal")
    for i, bits in enumerate(order):
        at = slice(i * CAP, (i + 1) * CAP)
        out_ref[me ^ bits, :, :depth] = numerator[at].astype(jnp.bfloat16)
        out_ref[me ^ bits, :, depth:] = tail[at].astype(jnp.bfloat16)


def pool(order, listed, own, other, gallery, block):
    rows, depth = gallery.shape
    slots = listed.shape[0]
    return pl.pallas_call(
        functools.partial(pool_kernel, order),
        out_shape=pltpu.VMEM((len(order), CAP, depth + LANES), jnp.bfloat16),
        in_specs=[VMEM] * 5,
        out_specs=VMEM,
        scratch_shapes=[pltpu.VMEM((slots, rows), jnp.bfloat16)],
        compiler_params=PARAMS,
        name="pool",
    )(keep(listed), keep(own), other, keep(gallery), keep(block))


def finish_kernel(sums_ref, spread_ref, out_ref):
    depth = out_ref.shape[1]
    sums = jnp.concatenate([sums_ref[s].astype(jnp.float32) for s in range(sums_ref.shape[0])], axis=0)
    sums = jnp.dot(
        spread_ref[...].astype(jnp.bfloat16), sums.astype(jnp.bfloat16), preferred_element_type=jnp.float32
    )
    out_ref[...] = sums[:, :depth] / (sums[:, depth : depth + 1] + sums[:, depth + 1 : depth + 2])


def finish(sums, spread):
    return pl.pallas_call(
        finish_kernel,
        out_shape=jax.ShapeDtypeStruct((spread.shape[0], sums.shape[2] - LANES), jnp.float32),
        in_specs=[VMEM, VMEM],
        out_specs=VMEM,
        compiler_params=PARAMS,
        name="finish",
    )(sums, keep(spread))


def join_kernel(*refs):
    *pieces, out_ref = refs
    row = 0
    for piece in pieces:
        out_ref[row : row + piece.shape[0], :] = piece[...]
        row += piece.shape[0]


def join(pieces):
    rows = sum(piece.shape[0] for piece in pieces)
    return pl.pallas_call(
        join_kernel,
        out_shape=pltpu.VMEM((rows, pieces[0].shape[1]), pieces[0].dtype),
        in_specs=[VMEM] * len(pieces),
        out_specs=VMEM,
        compiler_params=PARAMS,
        name="join",
    )(*pieces)


def swap(value, axis, size, bit):
    return lax.ppermute(value, axis, [(i, i ^ bit) for i in range(size)])


def body(devices, banks, bank_queries, gallery, test_queries, test_slabs, test_offsets):
    bank_own, test_own = bank_queries.shape[0], test_queries.shape[0]

    rounds = [[1 << k | 1] for k in range(devices.bit_length() - 2, 2, -1)] + [[5, 3], [1]]
    masks = [mask for masks in rounds for mask in masks]
    order = [0]
    for mask in masks:
        order = order + [o ^ mask for o in order]

    packed = pack(bank_queries, test_queries)
    other = swap(packed, "gal", devices, rounds[0][0])
    gallery, scale, packed, pick, block, spread = load(
        masks, bank_own, test_own, gallery, packed, test_slabs.T, test_offsets.T
    )
    others = [other]
    for near in rounds[1:]:
        packed = join([packed, *others])
        toward = near if len(near) == 1 else [near[0], near[1], near[0] ^ near[1]]
        others = [swap(packed, "gal", devices, mask) for mask in toward]
    other = others[0]

    colsum, listed = score(packed, other, pick, gallery, scale, block)
    bit = banks // 2
    other = jnp.zeros_like(colsum)
    while bit:
        other = swap(colsum, "bank", banks, bit)
        bit //= 2
        if bit:
            colsum = colsum + other
    sums = pool(order, listed, colsum, other, gallery, block)
    sums = lax.all_to_all(sums, "gal", 0, 0, tiled=True)
    return finish(sums, spread)


def solution(mesh):
    in_specs = (
        P(("bank", "gal"), None),
        P("gal", None),
        P(("bank", "gal"), None),
        P("bank", None),
        P("bank", None),
    )
    out_specs = P(("bank", "gal"), None)
    local = functools.partial(body, mesh.shape["gal"], mesh.shape["bank"])
    return jax.shard_map(local, mesh=mesh, in_specs=in_specs, out_specs=out_specs, check_vma=False)
```

```python
import functools

import jax
import jax.numpy as jnp
from jax import lax
from jax.experimental import pallas as pl
from jax.experimental.pallas import tpu as pltpu
from jax.sharding import PartitionSpec as P

BLOCK = 128
CHUNKS = 8
LANES = 128
CAP = 2
SHARPNESS = 20.0
LOG2E = 1.4426950408889634
epsilon = 1e-06

VMEM = pl.BlockSpec(memory_space=pltpu.VMEM)
HBM = pl.BlockSpec(memory_space=pltpu.HBM)
PARAMS = pltpu.CompilerParams(vmem_limit_bytes=16 << 20)


def in_hbm(value):
    return pltpu.with_memory_space_constraint(value, pltpu.HBM)


def keep(value):
    return pltpu.with_memory_space_constraint(value, pltpu.VMEM)


def pack_kernel(bank_hbm, test_hbm, packed_ref, bank_ref, test_ref, sems):
    copies = [
        pltpu.make_async_copy(bank_hbm, bank_ref, sems.at[0]),
        pltpu.make_async_copy(test_hbm, test_ref, sems.at[1]),
    ]
    for copy in copies:
        copy.start()
    for copy in copies:
        copy.wait()
    rows = bank_ref.shape[0]
    packed_ref[:rows, :] = bank_ref[...]
    packed_ref[rows:, :] = test_ref[...]


def pack(bank, test):
    return pl.pallas_call(
        pack_kernel,
        out_shape=pltpu.VMEM((bank.shape[0] + test.shape[0], bank.shape[1]), bank.dtype),
        in_specs=[HBM, HBM],
        out_specs=VMEM,
        scratch_shapes=[
            pltpu.VMEM(bank.shape, bank.dtype),
            pltpu.VMEM(test.shape, test.dtype),
            pltpu.SemaphoreType.DMA((2,)),
        ],
        compiler_params=PARAMS,
        name="pack",
    )(in_hbm(bank), in_hbm(test))


def bits_of(index, masks):
    value = jnp.zeros_like(index)
    for k, mask in enumerate(masks):
        value = value ^ jnp.where((index >> k) & 1 == 1, mask, 0)
    return value


def iota(shape, axis):
    return lax.broadcasted_iota(jnp.int32, shape, axis)


def route(masks, test_own, slabs, offsets, pick_ref, block_ref, spread_ref):
    me = lax.axis_index("gal")
    devices = 1 << len(masks)
    group = devices * test_own
    slots = devices * CAP

    found = jnp.sum(jnp.where(slabs == me, offsets + 1, 0), axis=0, keepdims=True)
    before = (iota((group, group), 0) // test_own == iota((group, group), 1) // test_own) & (
        iota((group, group), 0) < iota((group, group), 1)
    )
    flags = jnp.broadcast_to(jnp.where(found > 0, 1.0, 0.0), (8, group)).astype(jnp.bfloat16)
    rank = jnp.dot(flags, jnp.where(before, 1.0, 0.0).astype(jnp.bfloat16), preferred_element_type=jnp.float32)
    rank = rank[:1].astype(jnp.int32)
    index = iota((slots, group), 0)
    column = iota((slots, group), 1)
    filled = (column // test_own == me ^ bits_of(index // CAP, masks)) & (found > 0) & (rank == index % CAP)
    block = jnp.sum(jnp.where(filled, found, 0), axis=1, keepdims=True) - 1
    block_ref[...] = jnp.broadcast_to(block, block_ref.shape)
    from_row = jnp.sum(jnp.where(filled, column % test_own + 1, 0), axis=1, keepdims=True)
    index = iota((slots, 1), 0) // CAP
    slot_from = jnp.where(from_row > 0, index * test_own - 1 + from_row, -1)
    half = pick_ref.shape[2]
    for h in range(2):
        column = iota((slots, half), 1) + h * half
        pick_ref[h] = jnp.where(column == slot_from, 1.0, 0.0).astype(jnp.bfloat16)

    lane = iota((1, slots), 1)
    filled_before = jnp.zeros((1, slots), jnp.int32)
    mine = iota(slabs.shape, 1)
    for r in range(test_own):
        listed = jnp.sum(jnp.where(mine == me * test_own + r, slabs, 0), axis=1, keepdims=True)
        here = jnp.sum(jnp.where(listed == lane // CAP, 1, 0), axis=0, keepdims=True)
        spread_ref[r : r + 1, :] = jnp.where((here > 0) & (filled_before == lane % CAP), 1.0, 0.0)
        filled_before = filled_before + here


def load_kernel(
    masks, test_own, gallery_hbm, packed_ref, slabs_hbm, offsets_hbm,
    gallery_ref, turned_ref, scale_ref, packed_out, pick_ref, block_ref, spread_ref, slabs_ref, offsets_ref, sems, small_sems,
):
    rows, depth = gallery_hbm.shape
    part = rows // CHUNKS
    small = [
        pltpu.make_async_copy(slabs_hbm, slabs_ref, small_sems.at[0]),
        pltpu.make_async_copy(offsets_hbm, offsets_ref, small_sems.at[1]),
    ]
    copies = [
        pltpu.make_async_copy(
            gallery_hbm.at[pl.ds(c * part, part)], gallery_ref.at[pl.ds(c * part, part)], sems.at[c]
        )
        for c in range(CHUNKS)
    ]
    for copy in small + copies:
        copy.start()
    packed_out[...] = packed_ref[...]
    for c in range(CHUNKS):
        copies[c].wait()
        if c == 7:
            for copy in small:
                copy.wait()
            route(masks, test_own, slabs_ref[...], offsets_ref[...], pick_ref, block_ref, spread_ref)
        turned = gallery_ref[pl.ds(c * part, part), :].T
        turned_ref[:, c * part : (c + 1) * part] = turned
        values = turned.astype(jnp.float32)
        scale_ref[c : c + 1, :] = lax.rsqrt(jnp.sum(values * values, axis=0, keepdims=True) + epsilon)


def load(masks, test_own, gallery, packed, slabs, offsets):
    rows, depth = gallery.shape
    devices = 1 << len(masks)
    slots = devices * CAP
    return pl.pallas_call(
        functools.partial(load_kernel, masks, test_own),
        out_shape=(
            pltpu.VMEM(gallery.shape, gallery.dtype),
            pltpu.VMEM((depth, rows), gallery.dtype),
            pltpu.VMEM((CHUNKS, rows // CHUNKS), jnp.float32),
            pltpu.VMEM(packed.shape, packed.dtype),
            pltpu.VMEM((2, slots, devices * test_own // 2), jnp.bfloat16),
            pltpu.VMEM((slots, LANES), jnp.int32),
            pltpu.VMEM((test_own, slots), jnp.float32),
        ),
        in_specs=[HBM, VMEM, HBM, HBM],
        out_specs=(VMEM,) * 7,
        scratch_shapes=[
            pltpu.VMEM(slabs.shape, slabs.dtype),
            pltpu.VMEM(offsets.shape, offsets.dtype),
            pltpu.SemaphoreType.DMA((CHUNKS,)),
            pltpu.SemaphoreType.DMA((2,)),
        ],
        compiler_params=PARAMS,
        name="load",
    )(in_hbm(gallery), packed, in_hbm(slabs), in_hbm(offsets))


def scales(wide):
    return lax.rsqrt(jnp.sum(wide * wide, axis=1, keepdims=True) + epsilon) * (SHARPNESS * LOG2E)


def bank_kernel(bank_rows, first_ref, second_ref, turned_ref, scale_ref, colsum_ref):
    queries = jnp.concatenate([first_ref[:bank_rows], second_ref[:bank_rows]], axis=0)
    query_scale = scales(queries.astype(jnp.float32))
    part = scale_ref.shape[1]
    for c in range(CHUNKS):
        scores = jnp.dot(queries, turned_ref[:, c * part : (c + 1) * part], preferred_element_type=jnp.float32)
        exps = jnp.exp2(scores * scale_ref[c : c + 1, :] * query_scale)
        colsum_ref[c : c + 1, :] = jnp.sum(exps, axis=0, keepdims=True)


def score_bank(bank_rows, first, second, turned, scale):
    return pl.pallas_call(
        functools.partial(bank_kernel, bank_rows),
        out_shape=pltpu.VMEM(scale.shape, jnp.float32),
        in_specs=[VMEM] * 4,
        out_specs=VMEM,
        compiler_params=PARAMS,
        name="score_bank",
    )(keep(first), second, keep(turned), keep(scale))


def test_kernel(
    bank_rows, first_ref, second_ref, pick_ref, turned_ref, scale_ref, block_ref, colsum_ref, listed_ref, colsum_out
):
    colsum_out[...] = colsum_ref[...]
    wide = jnp.dot(pick_ref[0], first_ref[bank_rows:], preferred_element_type=jnp.float32)
    wide = wide + jnp.dot(pick_ref[1], second_ref[bank_rows:], preferred_element_type=jnp.float32)
    queries = wide.astype(jnp.bfloat16)
    part = scale_ref.shape[1]
    block = block_ref[...]
    picked = jnp.zeros(listed_ref.shape, jnp.float32)
    for c in range(CHUNKS):
        scores = jnp.dot(queries, turned_ref[:, c * part : (c + 1) * part], preferred_element_type=jnp.float32)
        scores = scores * scale_ref[c : c + 1, :]
        for b in range(part // BLOCK):
            picked = jnp.where(block == c * (part // BLOCK) + b, scores[:, b * BLOCK : (b + 1) * BLOCK], picked)
    listed_ref[...] = jnp.exp2(picked * scales(wide))


def score_tests(bank_rows, first, second, pick, turned, scale, block, colsum):
    return pl.pallas_call(
        functools.partial(test_kernel, bank_rows),
        out_shape=(pltpu.VMEM((block.shape[0], BLOCK), jnp.float32), pltpu.VMEM(colsum.shape, jnp.float32)),
        in_specs=[VMEM] * 7,
        out_specs=(VMEM, VMEM),
        compiler_params=PARAMS,
        name="score_tests",
    )(keep(first), keep(second), keep(pick), keep(turned), keep(scale), keep(block), keep(colsum))


def pool_kernel(order, listed_ref, own_ref, other_ref, gallery_ref, block_ref, out_ref, weight_ref):
    block = block_ref[...]
    slots = block.shape[0]
    rows, depth = gallery_ref.shape
    each = rows // BLOCK // CHUNKS
    inverse = 1.0 / (own_ref[...] + other_ref[...])
    picked = jnp.zeros((slots, BLOCK), jnp.float32)
    for b in range(rows // BLOCK):
        c, at = b // each, (b % each) * BLOCK
        picked = jnp.where(block == b, inverse[c : c + 1, at : at + BLOCK], picked)
    weight = listed_ref[...] * picked
    total = jnp.sum(weight, axis=1, keepdims=True)
    for b in range(rows // BLOCK):
        weight_ref[:, b * BLOCK : (b + 1) * BLOCK] = jnp.where(block == b, weight, 0.0).astype(jnp.bfloat16)
    numerator = jnp.dot(weight_ref[...], gallery_ref[...], preferred_element_type=jnp.float32)
    high = total.astype(jnp.bfloat16).astype(jnp.float32)
    lane = iota((slots, LANES), 1)
    tail = jnp.where(lane == 0, high, jnp.where(lane == 1, total - high, 0.0))
    me = lax.axis_index("gal")
    for i, bits in enumerate(order):
        at = slice(i * CAP, (i + 1) * CAP)
        out_ref[me ^ bits, :, :depth] = numerator[at].astype(jnp.bfloat16)
        out_ref[me ^ bits, :, depth:] = tail[at].astype(jnp.bfloat16)


def pool(order, listed, own, other, gallery, block):
    rows, depth = gallery.shape
    slots = listed.shape[0]
    return pl.pallas_call(
        functools.partial(pool_kernel, order),
        out_shape=pltpu.VMEM((len(order), CAP, depth + LANES), jnp.bfloat16),
        in_specs=[VMEM] * 5,
        out_specs=VMEM,
        scratch_shapes=[pltpu.VMEM((slots, rows), jnp.bfloat16)],
        compiler_params=PARAMS,
        name="pool",
    )(keep(listed), keep(own), other, keep(gallery), keep(block))


def finish_kernel(sums_ref, spread_ref, out_ref):
    depth = out_ref.shape[1]
    sums = jnp.concatenate([sums_ref[s].astype(jnp.float32) for s in range(sums_ref.shape[0])], axis=0)
    sums = jnp.dot(
        spread_ref[...].astype(jnp.bfloat16), sums.astype(jnp.bfloat16), preferred_element_type=jnp.float32
    )
    out_ref[...] = sums[:, :depth] / (sums[:, depth : depth + 1] + sums[:, depth + 1 : depth + 2])


def finish(sums, spread):
    return pl.pallas_call(
        finish_kernel,
        out_shape=jax.ShapeDtypeStruct((spread.shape[0], sums.shape[2] - LANES), jnp.float32),
        in_specs=[VMEM, VMEM],
        out_specs=VMEM,
        compiler_params=PARAMS,
        name="finish",
    )(sums, keep(spread))


def join_kernel(bank_own, own, *refs):
    *pieces, out_ref = refs
    bank, test = 0, sum(piece.shape[0] for piece in pieces) // own * bank_own
    for piece in pieces:
        rows = piece.shape[0]
        split = rows // own * bank_own
        out_ref[bank : bank + split, :] = piece[:split]
        out_ref[test : test + rows - split, :] = piece[split:]
        bank, test = bank + split, test + rows - split


def join(bank_own, test_own, pieces):
    rows = sum(piece.shape[0] for piece in pieces)
    return pl.pallas_call(
        functools.partial(join_kernel, bank_own, bank_own + test_own),
        out_shape=pltpu.VMEM((rows, pieces[0].shape[1]), pieces[0].dtype),
        in_specs=[VMEM] * len(pieces),
        out_specs=VMEM,
        compiler_params=PARAMS,
        name="join",
    )(*pieces)


def swap(value, axis, size, bit):
    return lax.ppermute(value, axis, [(i, i ^ bit) for i in range(size)])


def body(devices, banks, bank_queries, gallery, test_queries, test_slabs, test_offsets):
    bank_own, test_own = bank_queries.shape[0], test_queries.shape[0]

    rounds = [[1 << k | 1] for k in range(devices.bit_length() - 2, 2, -1)] + [[5, 3], [1]]
    masks = [mask for masks in rounds for mask in masks]
    order = [0]
    for mask in masks:
        order = order + [o ^ mask for o in order]

    packed = pack(bank_queries, test_queries)
    other = swap(packed, "gal", devices, rounds[0][0])
    gallery, turned, scale, packed, pick, block, spread = load(
        masks, test_own, gallery, packed, test_slabs.T, test_offsets.T
    )
    others = [other]
    for near in rounds[1:]:
        packed = join(bank_own, test_own, [packed, *others])
        toward = near if len(near) == 1 else [near[0], near[1], near[0] ^ near[1]]
        others = [swap(packed, "gal", devices, mask) for mask in toward]
    other = others[0]

    bank_rows = devices // 2 * bank_own
    first, second = packed, other
    colsum = score_bank(bank_rows, first, second, turned, scale)
    bit = banks // 2
    other = jnp.zeros_like(colsum)
    while bit:
        other = swap(colsum, "bank", banks, bit)
        bit //= 2
        if bit:
            colsum = colsum + other
    listed, colsum = score_tests(bank_rows, first, second, pick, turned, scale, block, colsum)
    sums = pool(order, listed, colsum, other, gallery, block)
    sums = lax.all_to_all(sums, "gal", 0, 0, tiled=True)
    return finish(sums, spread)


def solution(mesh):
    in_specs = (
        P(("bank", "gal"), None),
        P("gal", None),
        P(("bank", "gal"), None),
        P("bank", None),
        P("bank", None),
    )
    out_specs = P(("bank", "gal"), None)
    local = functools.partial(body, mesh.shape["gal"], mesh.shape["bank"])
    return jax.shard_map(local, mesh=mesh, in_specs=in_specs, out_specs=out_specs, check_vma=False)
```

```python
import functools

import jax
import jax.numpy as jnp
from jax import lax
from jax.experimental import pallas as pl
from jax.experimental.pallas import tpu as pltpu
from jax.sharding import PartitionSpec as P

BLOCK = 128
CHUNKS = 8
EARLY = 5
LANES = 128
CAP = 2
SHARPNESS = 20.0
LOG2E = 1.4426950408889634
epsilon = 1e-06

VMEM = pl.BlockSpec(memory_space=pltpu.VMEM)
HBM = pl.BlockSpec(memory_space=pltpu.HBM)
PARAMS = pltpu.CompilerParams(vmem_limit_bytes=16 << 20)


def in_hbm(value):
    return pltpu.with_memory_space_constraint(value, pltpu.HBM)


def keep(value):
    return pltpu.with_memory_space_constraint(value, pltpu.VMEM)


def bits_of(index, order):
    value = jnp.zeros_like(index)
    for place, mask in enumerate(order):
        value = jnp.where(index == place, mask, value)
    return value


def iota(shape, axis):
    return lax.broadcasted_iota(jnp.int32, shape, axis)


def route(order, test_own, slabs, offsets, pick_ref, block_ref, spread_ref):
    me = lax.axis_index("gal")
    devices = len(order)
    group = devices * test_own
    slots = devices * CAP

    found = jnp.sum(jnp.where(slabs == me, offsets + 1, 0), axis=0, keepdims=True)
    before = (iota((group, group), 0) // test_own == iota((group, group), 1) // test_own) & (
        iota((group, group), 0) < iota((group, group), 1)
    )
    flags = jnp.broadcast_to(jnp.where(found > 0, 1.0, 0.0), (8, group)).astype(jnp.bfloat16)
    rank = jnp.dot(flags, jnp.where(before, 1.0, 0.0).astype(jnp.bfloat16), preferred_element_type=jnp.float32)
    rank = rank[:1].astype(jnp.int32)
    index = iota((slots, group), 0)
    column = iota((slots, group), 1)
    filled = (column // test_own == me ^ bits_of(index // CAP, order)) & (found > 0) & (rank == index % CAP)
    block = jnp.sum(jnp.where(filled, found, 0), axis=1, keepdims=True) - 1
    block_ref[...] = jnp.broadcast_to(block, block_ref.shape)
    from_row = jnp.sum(jnp.where(filled, column % test_own + 1, 0), axis=1, keepdims=True)
    index = iota((slots, 1), 0) // CAP
    slot_from = jnp.where(from_row > 0, index * test_own - 1 + from_row, -1)
    half = pick_ref.shape[2]
    for h in range(2):
        column = iota((slots, half), 1) + h * half
        pick_ref[h] = jnp.where(column == slot_from, 1.0, 0.0).astype(jnp.bfloat16)

    lane = iota((1, slots), 1)
    filled_before = jnp.zeros((1, slots), jnp.int32)
    mine = iota(slabs.shape, 1)
    for r in range(test_own):
        listed = jnp.sum(jnp.where(mine == me * test_own + r, slabs, 0), axis=1, keepdims=True)
        here = jnp.sum(jnp.where(listed == lane // CAP, 1, 0), axis=0, keepdims=True)
        spread_ref[r : r + 1, :] = jnp.where((here > 0) & (filled_before == lane % CAP), 1.0, 0.0)
        filled_before = filled_before + here


def turn(gallery_hbm, first_row, gallery_ref, turned_ref, scale_ref, sems):
    parts, part = scale_ref.shape
    copies = [
        pltpu.make_async_copy(
            gallery_hbm.at[pl.ds(first_row + c * part, part)], gallery_ref.at[pl.ds(c * part, part)], sems.at[c]
        )
        for c in range(parts)
    ]
    for copy in copies:
        copy.start()

    def step(c):
        copies[c].wait()
        turned = gallery_ref[pl.ds(c * part, part), :].T
        turned_ref[:, c * part : (c + 1) * part] = turned
        values = turned.astype(jnp.float32)
        scale_ref[c : c + 1, :] = lax.rsqrt(jnp.sum(values * values, axis=0, keepdims=True) + epsilon)

    return [functools.partial(step, c) for c in range(parts)]


def low_kernel(
    gallery_hbm, bank_hbm, test_hbm, slabs_hbm, offsets_hbm,
    gallery_ref, turned_ref, scale_ref, bank_ref, test_ref, slabs_ref, offsets_ref, sems, small_sems,
):
    pairs = ((bank_hbm, bank_ref), (test_hbm, test_ref), (slabs_hbm, slabs_ref), (offsets_hbm, offsets_ref))
    small = [pltpu.make_async_copy(*pair, small_sems.at[i]) for i, pair in enumerate(pairs)]
    for copy in small:
        copy.start()
    steps = turn(gallery_hbm, 0, gallery_ref, turned_ref, scale_ref, sems)
    for step in steps:
        step()
    for copy in small:
        copy.wait()


def high_kernel(gallery_hbm, packed_ref, gallery_ref, turned_ref, scale_ref, packed_out, sems):
    steps = turn(gallery_hbm, gallery_hbm.shape[0] - gallery_ref.shape[0], gallery_ref, turned_ref, scale_ref, sems)
    packed_out[...] = packed_ref[...]
    for step in steps:
        step()


def part_shapes(gallery, parts):
    rows, depth = gallery.shape
    part = rows // CHUNKS
    return (
        pltpu.VMEM((parts * part, depth), gallery.dtype),
        pltpu.VMEM((depth, parts * part), gallery.dtype),
        pltpu.VMEM((parts, part), jnp.float32),
    )


def load_low(gallery, *small):
    return pl.pallas_call(
        low_kernel,
        out_shape=(*part_shapes(gallery, EARLY), *(pltpu.VMEM(x.shape, x.dtype) for x in small)),
        in_specs=[HBM] * 5,
        out_specs=(VMEM,) * 7,
        scratch_shapes=[pltpu.SemaphoreType.DMA((EARLY,)), pltpu.SemaphoreType.DMA((4,))],
        compiler_params=PARAMS,
        name="load_low",
    )(*map(in_hbm, (gallery, *small)))


def load_high(gallery, packed):
    return pl.pallas_call(
        high_kernel,
        out_shape=(*part_shapes(gallery, CHUNKS - EARLY), pltpu.VMEM(packed.shape, packed.dtype)),
        in_specs=[HBM, VMEM],
        out_specs=(VMEM,) * 4,
        scratch_shapes=[pltpu.SemaphoreType.DMA((CHUNKS - EARLY,))],
        compiler_params=PARAMS,
        name="load_high",
    )(in_hbm(gallery), packed)


def scales(wide):
    return lax.rsqrt(jnp.sum(wide * wide, axis=1, keepdims=True) + epsilon) * (SHARPNESS * LOG2E)


def chunk(c, turned_refs, scale_refs):
    part = scale_refs[0].shape[1]
    late, c = (0, c) if c < EARLY else (1, c - EARLY)
    return turned_refs[late][:, c * part : (c + 1) * part], scale_refs[late][c : c + 1, :]


def bank_kernel(bank_rows, first_ref, second_ref, low_ref, high_ref, low_scale_ref, high_scale_ref, colsum_ref):
    queries = jnp.concatenate([first_ref[:bank_rows], second_ref[:bank_rows]], axis=0)
    query_scale = scales(queries.astype(jnp.float32))
    for c in range(CHUNKS):
        turned, scale = chunk(c, (low_ref, high_ref), (low_scale_ref, high_scale_ref))
        scores = jnp.dot(queries, turned, preferred_element_type=jnp.float32)
        exps = jnp.exp2(scores * scale * query_scale)
        colsum_ref[c : c + 1, :] = jnp.sum(exps, axis=0, keepdims=True)


def score_bank(bank_rows, first, second, turned, scale):
    return pl.pallas_call(
        functools.partial(bank_kernel, bank_rows),
        out_shape=pltpu.VMEM((CHUNKS, scale[0].shape[1]), jnp.float32),
        in_specs=[VMEM] * 6,
        out_specs=VMEM,
        compiler_params=PARAMS,
        name="score_bank",
    )(keep(first), second, *map(keep, turned), *map(keep, scale))


def test_kernel(
    order, bank_rows, first_ref, second_ref, low_ref, high_ref, low_scale_ref, high_scale_ref,
    slabs_ref, offsets_ref, colsum_ref, listed_ref, block_ref, spread_ref, colsum_out, pick_ref,
):
    colsum_out[...] = colsum_ref[...]
    route(order, spread_ref.shape[0], slabs_ref[...], offsets_ref[...], pick_ref, block_ref, spread_ref)
    wide = jnp.dot(pick_ref[0], first_ref[bank_rows:], preferred_element_type=jnp.float32)
    wide = wide + jnp.dot(pick_ref[1], second_ref[bank_rows:], preferred_element_type=jnp.float32)
    queries = wide.astype(jnp.bfloat16)
    part = low_scale_ref.shape[1]
    block = block_ref[...]
    picked = jnp.zeros(listed_ref.shape, jnp.float32)
    for c in range(CHUNKS):
        turned, scale = chunk(c, (low_ref, high_ref), (low_scale_ref, high_scale_ref))
        scores = jnp.dot(queries, turned, preferred_element_type=jnp.float32) * scale
        for b in range(part // BLOCK):
            picked = jnp.where(block == c * (part // BLOCK) + b, scores[:, b * BLOCK : (b + 1) * BLOCK], picked)
    listed_ref[...] = jnp.exp2(picked * scales(wide))


def score_tests(order, bank_rows, first, second, turned, scale, slabs, offsets, colsum):
    slots = len(order) * CAP
    group = slabs.shape[1]
    return pl.pallas_call(
        functools.partial(test_kernel, order, bank_rows),
        out_shape=(
            pltpu.VMEM((slots, BLOCK), jnp.float32),
            pltpu.VMEM((slots, LANES), jnp.int32),
            pltpu.VMEM((group // len(order), slots), jnp.float32),
            pltpu.VMEM(colsum.shape, jnp.float32),
        ),
        in_specs=[VMEM] * 9,
        out_specs=(VMEM,) * 4,
        scratch_shapes=[pltpu.VMEM((2, slots, group // 2), jnp.bfloat16)],
        compiler_params=PARAMS,
        name="score_tests",
    )(*map(keep, (first, second, *turned, *scale, slabs, offsets, colsum)))


def pool_kernel(order, listed_ref, own_ref, other_ref, low_ref, high_ref, block_ref, out_ref, weight_ref):
    block = block_ref[...]
    slots = block.shape[0]
    early, depth = low_ref.shape
    rows = early + high_ref.shape[0]
    each = rows // BLOCK // CHUNKS
    inverse = 1.0 / (own_ref[...] + other_ref[...])
    picked = jnp.zeros((slots, BLOCK), jnp.float32)
    for b in range(rows // BLOCK):
        c, at = b // each, (b % each) * BLOCK
        picked = jnp.where(block == b, inverse[c : c + 1, at : at + BLOCK], picked)
    weight = listed_ref[...] * picked
    total = jnp.sum(weight, axis=1, keepdims=True)
    for b in range(rows // BLOCK):
        weight_ref[:, b * BLOCK : (b + 1) * BLOCK] = jnp.where(block == b, weight, 0.0).astype(jnp.bfloat16)
    numerator = jnp.dot(weight_ref[:, :early], low_ref[...], preferred_element_type=jnp.float32)
    numerator = numerator + jnp.dot(weight_ref[:, early:], high_ref[...], preferred_element_type=jnp.float32)
    high = total.astype(jnp.bfloat16).astype(jnp.float32)
    lane = iota((slots, LANES), 1)
    tail = jnp.where(lane == 0, high, jnp.where(lane == 1, total - high, 0.0))
    me = lax.axis_index("gal")
    for i, bits in enumerate(order):
        at = slice(i * CAP, (i + 1) * CAP)
        out_ref[me ^ bits, :, :depth] = numerator[at].astype(jnp.bfloat16)
        out_ref[me ^ bits, :, depth:] = tail[at].astype(jnp.bfloat16)


def pool(order, listed, own, other, gallery, block):
    depth = gallery[0].shape[1]
    rows = gallery[0].shape[0] + gallery[1].shape[0]
    slots = listed.shape[0]
    return pl.pallas_call(
        functools.partial(pool_kernel, order),
        out_shape=pltpu.VMEM((len(order), CAP, depth + LANES), jnp.bfloat16),
        in_specs=[VMEM] * 6,
        out_specs=VMEM,
        scratch_shapes=[pltpu.VMEM((slots, rows), jnp.bfloat16)],
        compiler_params=PARAMS,
        name="pool",
    )(keep(listed), keep(own), other, *map(keep, gallery), keep(block))


def finish_kernel(sums_ref, spread_ref, out_ref):
    depth = out_ref.shape[1]
    sums = jnp.concatenate([sums_ref[s].astype(jnp.float32) for s in range(sums_ref.shape[0])], axis=0)
    sums = jnp.dot(
        spread_ref[...].astype(jnp.bfloat16), sums.astype(jnp.bfloat16), preferred_element_type=jnp.float32
    )
    out_ref[...] = sums[:, :depth] / (sums[:, depth : depth + 1] + sums[:, depth + 1 : depth + 2])


def finish(sums, spread):
    return pl.pallas_call(
        finish_kernel,
        out_shape=jax.ShapeDtypeStruct((spread.shape[0], sums.shape[2] - LANES), jnp.float32),
        in_specs=[VMEM, VMEM],
        out_specs=VMEM,
        compiler_params=PARAMS,
        name="finish",
    )(sums, keep(spread))


def join_kernel(bank_own, own, *refs):
    *pieces, out_ref = refs
    bank, test = 0, sum(piece.shape[0] for piece in pieces) // own * bank_own
    for piece in pieces:
        rows = piece.shape[0]
        split = rows // own * bank_own
        out_ref[bank : bank + split, :] = piece[:split]
        out_ref[test : test + rows - split, :] = piece[split:]
        bank, test = bank + split, test + rows - split


def join(bank_own, test_own, pieces):
    rows = sum(piece.shape[0] for piece in pieces)
    return pl.pallas_call(
        functools.partial(join_kernel, bank_own, bank_own + test_own),
        out_shape=pltpu.VMEM((rows, pieces[0].shape[1]), pieces[0].dtype),
        in_specs=[VMEM] * len(pieces),
        out_specs=VMEM,
        compiler_params=PARAMS,
        name="join",
    )(*pieces)


def join_first(pieces):
    def kernel(*refs):
        *ins, out_ref = refs
        row = 0
        for piece in ins:
            out_ref[row : row + piece.shape[0], :] = piece[...]
            row += piece.shape[0]

    rows = sum(piece.shape[0] for piece in pieces)
    return pl.pallas_call(
        kernel,
        out_shape=pltpu.VMEM((rows, pieces[0].shape[1]), pieces[0].dtype),
        in_specs=[VMEM] * len(pieces),
        out_specs=VMEM,
        compiler_params=PARAMS,
        name="join",
    )(*pieces)


def swap(value, axis, size, bit):
    return lax.ppermute(value, axis, [(i, i ^ bit) for i in range(size)])


def body(devices, banks, bank_queries, gallery, test_queries, test_slabs, test_offsets):
    bank_own, test_own = bank_queries.shape[0], test_queries.shape[0]

    rounds = [[1 << k | 1] for k in range(devices.bit_length() - 2, 2, -1)] + [[3, 7, 4], [1]]
    order = [0]
    for masks in rounds:
        order = order + [o ^ mask for mask in masks for o in order]

    others = [swap(rows, "gal", devices, rounds[0][0]) for rows in (bank_queries, test_queries)]
    low, low_turned, low_scale, bank, test, slabs, offsets = load_low(
        gallery, bank_queries, test_queries, test_slabs.T, test_offsets.T
    )
    packed = join_first([bank, others[0], test, others[1]])
    for i, near in enumerate(rounds[1:]):
        if i:
            packed = join(bank_own, test_own, [packed, *others])
        others = [swap(packed, "gal", devices, mask) for mask in near]
        if i == 0:
            high, high_turned, high_scale, packed = load_high(gallery, packed)
    other = others[0]
    gallery, turned, scale = (low, high), (low_turned, high_turned), (low_scale, high_scale)

    bank_rows = devices // 2 * bank_own
    first, second = packed, other
    colsum = score_bank(bank_rows, first, second, turned, scale)
    bit = banks // 2
    other = jnp.zeros_like(colsum)
    while bit:
        other = swap(colsum, "bank", banks, bit)
        bit //= 2
        if bit:
            colsum = colsum + other
    listed, block, spread, colsum = score_tests(
        order, bank_rows, first, second, turned, scale, slabs, offsets, colsum
    )
    sums = pool(order, listed, colsum, other, gallery, block)
    sums = lax.all_to_all(sums, "gal", 0, 0, tiled=True)
    return finish(sums, spread)


def solution(mesh):
    in_specs = (
        P(("bank", "gal"), None),
        P("gal", None),
        P(("bank", "gal"), None),
        P("bank", None),
        P("bank", None),
    )
    out_specs = P(("bank", "gal"), None)
    local = functools.partial(body, mesh.shape["gal"], mesh.shape["bank"])
    return jax.shard_map(local, mesh=mesh, in_specs=in_specs, out_specs=out_specs, check_vma=False)
```

```python
import functools

import jax
import jax.numpy as jnp
from jax import lax
from jax.experimental import pallas as pl
from jax.experimental.pallas import tpu as pltpu
from jax.sharding import PartitionSpec as P

BLOCK = 128
CHUNKS = 8
PARTS = (4, 3, 1)
LANES = 128
CAP = 2
SHARPNESS = 20.0
LOG2E = 1.4426950408889634
epsilon = 1e-06

VMEM = pl.BlockSpec(memory_space=pltpu.VMEM)
HBM = pl.BlockSpec(memory_space=pltpu.HBM)
PARAMS = pltpu.CompilerParams(vmem_limit_bytes=16 << 20)


def in_hbm(value):
    return pltpu.with_memory_space_constraint(value, pltpu.HBM)


def keep(value):
    return pltpu.with_memory_space_constraint(value, pltpu.VMEM)


def bits_of(index, order):
    value = jnp.zeros_like(index)
    for place, mask in enumerate(order):
        value = jnp.where(index == place, mask, value)
    return value


def iota(shape, axis):
    return lax.broadcasted_iota(jnp.int32, shape, axis)


def route(order, test_own, slabs, offsets, pick_ref, block_ref, spread_ref):
    me = lax.axis_index("gal")
    devices = len(order)
    group = devices * test_own
    slots = devices * CAP

    found = jnp.sum(jnp.where(slabs == me, offsets + 1, 0), axis=0, keepdims=True)
    before = (iota((group, group), 0) // test_own == iota((group, group), 1) // test_own) & (
        iota((group, group), 0) < iota((group, group), 1)
    )
    flags = jnp.broadcast_to(jnp.where(found > 0, 1.0, 0.0), (8, group)).astype(jnp.bfloat16)
    rank = jnp.dot(flags, jnp.where(before, 1.0, 0.0).astype(jnp.bfloat16), preferred_element_type=jnp.float32)
    rank = rank[:1].astype(jnp.int32)
    index = iota((slots, group), 0)
    column = iota((slots, group), 1)
    filled = (column // test_own == me ^ bits_of(index // CAP, order)) & (found > 0) & (rank == index % CAP)
    block = jnp.sum(jnp.where(filled, found, 0), axis=1, keepdims=True) - 1
    block_ref[...] = jnp.broadcast_to(block, block_ref.shape)
    from_row = jnp.sum(jnp.where(filled, column % test_own + 1, 0), axis=1, keepdims=True)
    index = iota((slots, 1), 0) // CAP
    slot_from = jnp.where(from_row > 0, index * test_own - 1 + from_row, -1)
    half = pick_ref.shape[2]
    for h in range(2):
        column = iota((slots, half), 1) + h * half
        pick_ref[h] = jnp.where(column == slot_from, 1.0, 0.0).astype(jnp.bfloat16)

    lane = iota((1, slots), 1)
    filled_before = jnp.zeros((1, slots), jnp.int32)
    mine = iota(slabs.shape, 1)
    for r in range(test_own):
        listed = jnp.sum(jnp.where(mine == me * test_own + r, slabs, 0), axis=1, keepdims=True)
        here = jnp.sum(jnp.where(listed == lane // CAP, 1, 0), axis=0, keepdims=True)
        spread_ref[r : r + 1, :] = jnp.where((here > 0) & (filled_before == lane % CAP), 1.0, 0.0)
        filled_before = filled_before + here


def fetch(gallery_hbm, first_row, gallery_ref, sems):
    part = gallery_hbm.shape[0] // CHUNKS
    copies = [
        pltpu.make_async_copy(
            gallery_hbm.at[pl.ds(first_row + c * part, part)], gallery_ref.at[pl.ds(c * part, part)], sems.at[c]
        )
        for c in range(gallery_ref.shape[0] // part)
    ]
    for copy in copies:
        copy.start()
    return copies


def turn(c, at, gallery_ref, turned_ref, scale_ref):
    part = scale_ref.shape[1]
    turned = gallery_ref[pl.ds(at * part, part), :].T
    turned_ref[:, c * part : (c + 1) * part] = turned
    values = turned.astype(jnp.float32)
    scale_ref[c : c + 1, :] = lax.rsqrt(jnp.sum(values * values, axis=0, keepdims=True) + epsilon)


def low_kernel(
    gallery_hbm, bank_hbm, test_hbm, slabs_hbm, offsets_hbm,
    gallery_ref, turned_ref, scale_ref, bank_ref, test_ref, slabs_ref, offsets_ref, sems, small_sems,
):
    pairs = ((bank_hbm, bank_ref), (test_hbm, test_ref), (slabs_hbm, slabs_ref), (offsets_hbm, offsets_ref))
    small = [pltpu.make_async_copy(*pair, small_sems.at[i]) for i, pair in enumerate(pairs)]
    for copy in small:
        copy.start()
    for c, copy in enumerate(fetch(gallery_hbm, 0, gallery_ref, sems)):
        copy.wait()
        turn(c, c, gallery_ref, turned_ref, scale_ref)
    for copy in small:
        copy.wait()


def more_kernel(gallery_hbm, packed_ref, gallery_ref, turned_ref, scale_ref, packed_out, sems):
    copies = fetch(gallery_hbm, gallery_hbm.shape[0] - gallery_ref.shape[0], gallery_ref, sems)
    packed_out[...] = packed_ref[...]
    for c, copy in enumerate(copies):
        copy.wait()
        if c < scale_ref.shape[0]:
            turn(c, c, gallery_ref, turned_ref, scale_ref)


def last_kernel(gallery_ref, packed_ref, turned_ref, scale_ref, packed_out):
    packed_out[...] = packed_ref[...]
    for c in range(scale_ref.shape[0]):
        turn(c, PARTS[1] + c, gallery_ref, turned_ref, scale_ref)


def part_shapes(gallery, parts):
    rows, depth = gallery.shape
    part = rows // CHUNKS
    return (
        pltpu.VMEM((depth, parts * part), gallery.dtype),
        pltpu.VMEM((parts, part), jnp.float32),
    )


def rows_shape(gallery, parts):
    rows, depth = gallery.shape
    return pltpu.VMEM((rows // CHUNKS * parts, depth), gallery.dtype)


def load_low(gallery, *small):
    return pl.pallas_call(
        low_kernel,
        out_shape=(rows_shape(gallery, PARTS[0]), *part_shapes(gallery, PARTS[0]), *(pltpu.VMEM(x.shape, x.dtype) for x in small)),
        in_specs=[HBM] * 5,
        out_specs=(VMEM,) * 7,
        scratch_shapes=[pltpu.SemaphoreType.DMA((PARTS[0],)), pltpu.SemaphoreType.DMA((4,))],
        compiler_params=PARAMS,
        name="load_low",
    )(*map(in_hbm, (gallery, *small)))


def load_more(gallery, packed):
    parts = CHUNKS - PARTS[0]
    return pl.pallas_call(
        more_kernel,
        out_shape=(
            rows_shape(gallery, parts),
            *part_shapes(gallery, PARTS[1]),
            pltpu.VMEM(packed.shape, packed.dtype),
        ),
        in_specs=[HBM, VMEM],
        out_specs=(VMEM,) * 4,
        scratch_shapes=[pltpu.SemaphoreType.DMA((parts,))],
        compiler_params=PARAMS,
        name="load_more",
    )(in_hbm(gallery), packed)


def turn_last(gallery, more, packed):
    return pl.pallas_call(
        last_kernel,
        out_shape=(*part_shapes(gallery, PARTS[2]), pltpu.VMEM(packed.shape, packed.dtype)),
        in_specs=[VMEM, VMEM],
        out_specs=(VMEM,) * 3,
        compiler_params=PARAMS,
        name="turn_last",
    )(keep(more), packed)


def scales(wide):
    return lax.rsqrt(jnp.sum(wide * wide, axis=1, keepdims=True) + epsilon) * (SHARPNESS * LOG2E)


def chunks(turned_refs, scale_refs):
    for turned_ref, scale_ref in zip(turned_refs, scale_refs):
        parts, part = scale_ref.shape
        for c in range(parts):
            yield turned_ref[:, c * part : (c + 1) * part], scale_ref[c : c + 1, :]


def bank_kernel(bank_rows, first_ref, second_ref, *refs):
    number = len(PARTS)
    turned_refs, scale_refs, colsum_ref = refs[:number], refs[number : 2 * number], refs[-1]
    queries = jnp.concatenate([first_ref[:bank_rows], second_ref[:bank_rows]], axis=0)
    query_scale = scales(queries.astype(jnp.float32))
    for c, (turned, scale) in enumerate(chunks(turned_refs, scale_refs)):
        scores = jnp.dot(queries, turned, preferred_element_type=jnp.float32)
        exps = jnp.exp2(scores * scale * query_scale)
        colsum_ref[c : c + 1, :] = jnp.sum(exps, axis=0, keepdims=True)


def score_bank(bank_rows, first, second, turned, scale):
    return pl.pallas_call(
        functools.partial(bank_kernel, bank_rows),
        out_shape=pltpu.VMEM((CHUNKS, scale[0].shape[1]), jnp.float32),
        in_specs=[VMEM] * (2 + 2 * len(PARTS)),
        out_specs=VMEM,
        compiler_params=PARAMS,
        name="score_bank",
    )(keep(first), second, *map(keep, turned), *map(keep, scale))


def test_kernel(order, bank_rows, first_ref, second_ref, *refs):
    number = len(PARTS)
    turned_refs, scale_refs, refs = refs[:number], refs[number : 2 * number], refs[2 * number :]
    slabs_ref, offsets_ref, colsum_ref, listed_ref, block_ref, spread_ref, colsum_out, pick_ref = refs
    colsum_out[...] = colsum_ref[...]
    route(order, spread_ref.shape[0], slabs_ref[...], offsets_ref[...], pick_ref, block_ref, spread_ref)
    wide = jnp.dot(pick_ref[0], first_ref[bank_rows:], preferred_element_type=jnp.float32)
    wide = wide + jnp.dot(pick_ref[1], second_ref[bank_rows:], preferred_element_type=jnp.float32)
    queries = wide.astype(jnp.bfloat16)
    part = scale_refs[0].shape[1]
    block = block_ref[...]
    picked = jnp.zeros(listed_ref.shape, jnp.float32)
    for c, (turned, scale) in enumerate(chunks(turned_refs, scale_refs)):
        scores = jnp.dot(queries, turned, preferred_element_type=jnp.float32) * scale
        for b in range(part // BLOCK):
            picked = jnp.where(block == c * (part // BLOCK) + b, scores[:, b * BLOCK : (b + 1) * BLOCK], picked)
    listed_ref[...] = jnp.exp2(picked * scales(wide))


def score_tests(order, bank_rows, first, second, turned, scale, slabs, offsets, colsum):
    slots = len(order) * CAP
    group = slabs.shape[1]
    return pl.pallas_call(
        functools.partial(test_kernel, order, bank_rows),
        out_shape=(
            pltpu.VMEM((slots, BLOCK), jnp.float32),
            pltpu.VMEM((slots, LANES), jnp.int32),
            pltpu.VMEM((group // len(order), slots), jnp.float32),
            pltpu.VMEM(colsum.shape, jnp.float32),
        ),
        in_specs=[VMEM] * (5 + 2 * len(PARTS)),
        out_specs=(VMEM,) * 4,
        scratch_shapes=[pltpu.VMEM((2, slots, group // 2), jnp.bfloat16)],
        compiler_params=PARAMS,
        name="score_tests",
    )(*map(keep, (first, second, *turned, *scale, slabs, offsets, colsum)))


def pool_kernel(order, listed_ref, own_ref, other_ref, block_ref, *refs):
    *gallery_refs, out_ref, weight_ref = refs
    block = block_ref[...]
    slots, rows = weight_ref.shape
    depth = gallery_refs[0].shape[1]
    each = rows // BLOCK // CHUNKS
    inverse = 1.0 / (own_ref[...] + other_ref[...])
    picked = jnp.zeros((slots, BLOCK), jnp.float32)
    for b in range(rows // BLOCK):
        c, at = b // each, (b % each) * BLOCK
        picked = jnp.where(block == b, inverse[c : c + 1, at : at + BLOCK], picked)
    weight = listed_ref[...] * picked
    total = jnp.sum(weight, axis=1, keepdims=True)
    for b in range(rows // BLOCK):
        weight_ref[:, b * BLOCK : (b + 1) * BLOCK] = jnp.where(block == b, weight, 0.0).astype(jnp.bfloat16)
    numerator, row = jnp.zeros((slots, depth), jnp.float32), 0
    for gallery_ref in gallery_refs:
        here = slice(row, row + gallery_ref.shape[0])
        numerator = numerator + jnp.dot(weight_ref[:, here], gallery_ref[...], preferred_element_type=jnp.float32)
        row = here.stop
    high = total.astype(jnp.bfloat16).astype(jnp.float32)
    lane = iota((slots, LANES), 1)
    tail = jnp.where(lane == 0, high, jnp.where(lane == 1, total - high, 0.0))
    me = lax.axis_index("gal")
    for i, bits in enumerate(order):
        at = slice(i * CAP, (i + 1) * CAP)
        out_ref[me ^ bits, :, :depth] = numerator[at].astype(jnp.bfloat16)
        out_ref[me ^ bits, :, depth:] = tail[at].astype(jnp.bfloat16)


def pool(order, listed, own, other, gallery, block):
    depth = gallery[0].shape[1]
    rows = sum(part.shape[0] for part in gallery)
    slots = listed.shape[0]
    return pl.pallas_call(
        functools.partial(pool_kernel, order),
        out_shape=pltpu.VMEM((len(order), CAP, depth + LANES), jnp.bfloat16),
        in_specs=[VMEM] * (4 + len(gallery)),
        out_specs=VMEM,
        scratch_shapes=[pltpu.VMEM((slots, rows), jnp.bfloat16)],
        compiler_params=PARAMS,
        name="pool",
    )(keep(listed), keep(own), other, keep(block), *map(keep, gallery))


def finish_kernel(sums_ref, spread_ref, out_ref):
    depth = out_ref.shape[1]
    sums = jnp.concatenate([sums_ref[s].astype(jnp.float32) for s in range(sums_ref.shape[0])], axis=0)
    sums = jnp.dot(
        spread_ref[...].astype(jnp.bfloat16), sums.astype(jnp.bfloat16), preferred_element_type=jnp.float32
    )
    out_ref[...] = sums[:, :depth] / (sums[:, depth : depth + 1] + sums[:, depth + 1 : depth + 2])


def finish(sums, spread):
    return pl.pallas_call(
        finish_kernel,
        out_shape=jax.ShapeDtypeStruct((spread.shape[0], sums.shape[2] - LANES), jnp.float32),
        in_specs=[VMEM, VMEM],
        out_specs=VMEM,
        compiler_params=PARAMS,
        name="finish",
    )(sums, keep(spread))


def join_kernel(bank_own, own, *refs):
    *pieces, out_ref = refs
    bank, test = 0, sum(piece.shape[0] for piece in pieces) // own * bank_own
    for piece in pieces:
        rows = piece.shape[0]
        split = rows // own * bank_own
        out_ref[bank : bank + split, :] = piece[:split]
        out_ref[test : test + rows - split, :] = piece[split:]
        bank, test = bank + split, test + rows - split


def join(bank_own, test_own, pieces):
    rows = sum(piece.shape[0] for piece in pieces)
    return pl.pallas_call(
        functools.partial(join_kernel, bank_own, bank_own + test_own),
        out_shape=pltpu.VMEM((rows, pieces[0].shape[1]), pieces[0].dtype),
        in_specs=[VMEM] * len(pieces),
        out_specs=VMEM,
        compiler_params=PARAMS,
        name="join",
    )(*pieces)


def join_first(pieces):
    def kernel(*refs):
        *ins, out_ref = refs
        row = 0
        for piece in ins:
            out_ref[row : row + piece.shape[0], :] = piece[...]
            row += piece.shape[0]

    rows = sum(piece.shape[0] for piece in pieces)
    return pl.pallas_call(
        kernel,
        out_shape=pltpu.VMEM((rows, pieces[0].shape[1]), pieces[0].dtype),
        in_specs=[VMEM] * len(pieces),
        out_specs=VMEM,
        compiler_params=PARAMS,
        name="join",
    )(*pieces)


def swap(value, axis, size, bit):
    return lax.ppermute(value, axis, [(i, i ^ bit) for i in range(size)])


def body(devices, banks, bank_queries, gallery, test_queries, test_slabs, test_offsets):
    bank_own, test_own = bank_queries.shape[0], test_queries.shape[0]

    rounds = [[1 << k | 1] for k in range(devices.bit_length() - 2, 2, -1)] + [[3, 7, 4], [1]]
    order = [0]
    for masks in rounds:
        order = order + [o ^ mask for mask in masks for o in order]

    others = [swap(rows, "gal", devices, rounds[0][0]) for rows in (bank_queries, test_queries)]
    low, low_turned, low_scale, bank, test, slabs, offsets = load_low(
        gallery, bank_queries, test_queries, test_slabs.T, test_offsets.T
    )
    packed = join_first([bank, others[0], test, others[1]])
    for i, near in enumerate(rounds[1:]):
        if i:
            packed = join(bank_own, test_own, [packed, *others])
        others = [swap(packed, "gal", devices, mask) for mask in near]
        if i == 0:
            more, more_turned, more_scale, packed = load_more(gallery, packed)
        if i == len(rounds) - 2:
            last_turned, last_scale, packed = turn_last(gallery, more, packed)
    other = others[0]
    turned, scale = (low_turned, more_turned, last_turned), (low_scale, more_scale, last_scale)
    gallery = (low, more)

    bank_rows = devices // 2 * bank_own
    first, second = packed, other
    colsum = score_bank(bank_rows, first, second, turned, scale)
    bit = banks // 2
    other = jnp.zeros_like(colsum)
    while bit:
        other = swap(colsum, "bank", banks, bit)
        bit //= 2
        if bit:
            colsum = colsum + other
    listed, block, spread, colsum = score_tests(
        order, bank_rows, first, second, turned, scale, slabs, offsets, colsum
    )
    sums = pool(order, listed, colsum, other, gallery, block)
    sums = lax.all_to_all(sums, "gal", 0, 0, tiled=True)
    return finish(sums, spread)


def solution(mesh):
    in_specs = (
        P(("bank", "gal"), None),
        P("gal", None),
        P(("bank", "gal"), None),
        P("bank", None),
        P("bank", None),
    )
    out_specs = P(("bank", "gal"), None)
    local = functools.partial(body, mesh.shape["gal"], mesh.shape["bank"])
    return jax.shard_map(local, mesh=mesh, in_specs=in_specs, out_specs=out_specs, check_vma=False)
```

```python
import functools

import jax
import jax.numpy as jnp
from jax import lax
from jax.experimental import pallas as pl
from jax.experimental.pallas import tpu as pltpu
from jax.sharding import PartitionSpec as P

BLOCK = 128
CHUNKS = 8
PARTS = (4, 3, 1)
LANES = 128
CAP = 2
SHARPNESS = 20.0
LOG2E = 1.4426950408889634
epsilon = 1e-06

VMEM = pl.BlockSpec(memory_space=pltpu.VMEM)
HBM = pl.BlockSpec(memory_space=pltpu.HBM)
PARAMS = pltpu.CompilerParams(vmem_limit_bytes=16 << 20)


def in_hbm(value):
    return pltpu.with_memory_space_constraint(value, pltpu.HBM)


def keep(value):
    return pltpu.with_memory_space_constraint(value, pltpu.VMEM)


def bits_of(index, order):
    value = jnp.zeros_like(index)
    for place, mask in enumerate(order):
        value = jnp.where(index == place, mask, value)
    return value


def iota(shape, axis):
    return lax.broadcasted_iota(jnp.int32, shape, axis)


def route(order, test_own, slabs, offsets, pick_ref, block_ref, spread_ref):
    me = lax.axis_index("gal")
    devices = len(order)
    group = devices * test_own
    slots = devices * CAP

    found = jnp.sum(jnp.where(slabs == me, offsets + 1, 0), axis=0, keepdims=True)
    before = (iota((group, group), 0) // test_own == iota((group, group), 1) // test_own) & (
        iota((group, group), 0) < iota((group, group), 1)
    )
    flags = jnp.broadcast_to(jnp.where(found > 0, 1.0, 0.0), (8, group)).astype(jnp.bfloat16)
    rank = jnp.dot(flags, jnp.where(before, 1.0, 0.0).astype(jnp.bfloat16), preferred_element_type=jnp.float32)
    rank = rank[:1].astype(jnp.int32)
    index = iota((slots, group), 0)
    column = iota((slots, group), 1)
    filled = (column // test_own == me ^ bits_of(index // CAP, order)) & (found > 0) & (rank == index % CAP)
    block = jnp.sum(jnp.where(filled, found, 0), axis=1, keepdims=True) - 1
    block_ref[...] = jnp.broadcast_to(block, block_ref.shape)
    from_row = jnp.sum(jnp.where(filled, column % test_own + 1, 0), axis=1, keepdims=True)
    index = iota((slots, 1), 0) // CAP
    slot_from = jnp.where(from_row > 0, index * test_own - 1 + from_row, -1)
    half = pick_ref.shape[2]
    for h in range(2):
        column = iota((slots, half), 1) + h * half
        pick_ref[h] = jnp.where(column == slot_from, 1.0, 0.0).astype(jnp.bfloat16)

    lane = iota((1, slots), 1)
    filled_before = jnp.zeros((1, slots), jnp.int32)
    mine = iota(slabs.shape, 1)
    for r in range(test_own):
        listed = jnp.sum(jnp.where(mine == me * test_own + r, slabs, 0), axis=1, keepdims=True)
        here = jnp.sum(jnp.where(listed == lane // CAP, 1, 0), axis=0, keepdims=True)
        spread_ref[r : r + 1, :] = jnp.where((here > 0) & (filled_before == lane % CAP), 1.0, 0.0)
        filled_before = filled_before + here


def fetch(gallery_hbm, first_row, gallery_ref, sems):
    part = gallery_hbm.shape[0] // CHUNKS
    copies = [
        pltpu.make_async_copy(
            gallery_hbm.at[pl.ds(first_row + c * part, part)], gallery_ref.at[pl.ds(c * part, part)], sems.at[c]
        )
        for c in range(gallery_ref.shape[0] // part)
    ]
    for copy in copies:
        copy.start()
    return copies


def turn(c, at, gallery_ref, turned_ref, scale_ref):
    part = scale_ref.shape[1]
    turned = gallery_ref[pl.ds(at * part, part), :].T
    turned_ref[:, c * part : (c + 1) * part] = turned
    values = turned.astype(jnp.float32)
    scale_ref[c : c + 1, :] = lax.rsqrt(jnp.sum(values * values, axis=0, keepdims=True) + epsilon)


def low_kernel(
    gallery_hbm, bank_hbm, test_hbm, slabs_hbm, offsets_hbm,
    gallery_ref, turned_ref, scale_ref, bank_ref, test_ref, slabs_ref, offsets_ref, sems, small_sems,
):
    pairs = ((bank_hbm, bank_ref), (test_hbm, test_ref), (slabs_hbm, slabs_ref), (offsets_hbm, offsets_ref))
    small = [pltpu.make_async_copy(*pair, small_sems.at[i]) for i, pair in enumerate(pairs)]
    for copy in small:
        copy.start()
    for c, copy in enumerate(fetch(gallery_hbm, 0, gallery_ref, sems)):
        copy.wait()
        turn(c, c, gallery_ref, turned_ref, scale_ref)
    for copy in small:
        copy.wait()


def more_kernel(gallery_hbm, packed_ref, gallery_ref, turned_ref, scale_ref, packed_out, sems):
    copies = fetch(gallery_hbm, gallery_hbm.shape[0] - gallery_ref.shape[0], gallery_ref, sems)
    packed_out[...] = packed_ref[...]
    for c, copy in enumerate(copies):
        copy.wait()
        if c < scale_ref.shape[0]:
            turn(c, c, gallery_ref, turned_ref, scale_ref)


def last_kernel(gallery_ref, packed_ref, turned_ref, scale_ref, packed_out):
    packed_out[...] = packed_ref[...]
    for c in range(scale_ref.shape[0]):
        turn(c, PARTS[1] + c, gallery_ref, turned_ref, scale_ref)


def part_shapes(gallery, parts):
    rows, depth = gallery.shape
    part = rows // CHUNKS
    return (
        pltpu.VMEM((depth, parts * part), gallery.dtype),
        pltpu.VMEM((parts, part), jnp.float32),
    )


def rows_shape(gallery, parts):
    rows, depth = gallery.shape
    return pltpu.VMEM((rows // CHUNKS * parts, depth), gallery.dtype)


def load_low(gallery, *small):
    return pl.pallas_call(
        low_kernel,
        out_shape=(rows_shape(gallery, PARTS[0]), *part_shapes(gallery, PARTS[0]), *(pltpu.VMEM(x.shape, x.dtype) for x in small)),
        in_specs=[HBM] * 5,
        out_specs=(VMEM,) * 7,
        scratch_shapes=[pltpu.SemaphoreType.DMA((PARTS[0],)), pltpu.SemaphoreType.DMA((4,))],
        compiler_params=PARAMS,
        name="load_low",
    )(*map(in_hbm, (gallery, *small)))


def load_more(gallery, packed):
    parts = CHUNKS - PARTS[0]
    return pl.pallas_call(
        more_kernel,
        out_shape=(
            rows_shape(gallery, parts),
            *part_shapes(gallery, PARTS[1]),
            pltpu.VMEM(packed.shape, packed.dtype),
        ),
        in_specs=[HBM, VMEM],
        out_specs=(VMEM,) * 4,
        scratch_shapes=[pltpu.SemaphoreType.DMA((parts,))],
        compiler_params=PARAMS,
        name="load_more",
    )(in_hbm(gallery), packed)


def turn_last(gallery, more, packed):
    return pl.pallas_call(
        last_kernel,
        out_shape=(*part_shapes(gallery, PARTS[2]), pltpu.VMEM(packed.shape, packed.dtype)),
        in_specs=[VMEM, VMEM],
        out_specs=(VMEM,) * 3,
        compiler_params=PARAMS,
        name="turn_last",
    )(keep(more), packed)


def scales(wide):
    return lax.rsqrt(jnp.sum(wide * wide, axis=1, keepdims=True) + epsilon) * (SHARPNESS * LOG2E)


def chunks(turned_refs, scale_refs):
    for turned_ref, scale_ref in zip(turned_refs, scale_refs):
        parts, part = scale_ref.shape
        for c in range(parts):
            yield turned_ref[:, c * part : (c + 1) * part], scale_ref[c : c + 1, :]


def bank_kernel(bank_rows, first_ref, second_ref, *refs):
    number = len(PARTS)
    turned_refs, scale_refs, colsum_ref = refs[:number], refs[number : 2 * number], refs[-1]
    queries = jnp.concatenate([first_ref[:bank_rows], second_ref[:bank_rows]], axis=0)
    query_scale = scales(queries.astype(jnp.float32))
    for c, (turned, scale) in enumerate(chunks(turned_refs, scale_refs)):
        scores = jnp.dot(queries, turned, preferred_element_type=jnp.float32)
        exps = jnp.exp2(scores * scale * query_scale)
        colsum_ref[c : c + 1, :] = jnp.sum(exps, axis=0, keepdims=True)


def score_bank(bank_rows, first, second, turned, scale):
    return pl.pallas_call(
        functools.partial(bank_kernel, bank_rows),
        out_shape=pltpu.VMEM((CHUNKS, scale[0].shape[1]), jnp.float32),
        in_specs=[VMEM] * (2 + 2 * len(PARTS)),
        out_specs=VMEM,
        compiler_params=PARAMS,
        name="score_bank",
    )(keep(first), second, *map(keep, turned), *map(keep, scale))


def test_kernel(order, bank_rows, first_ref, second_ref, *refs):
    number = len(PARTS)
    turned_refs, scale_refs, refs = refs[:number], refs[number : 2 * number], refs[2 * number :]
    slabs_ref, offsets_ref, colsum_ref, listed_ref, block_ref, spread_ref, colsum_out, pick_ref = refs
    colsum_out[...] = colsum_ref[...]
    route(order, spread_ref.shape[0], slabs_ref[...], offsets_ref[...], pick_ref, block_ref, spread_ref)
    wide = jnp.dot(pick_ref[0], first_ref[bank_rows:], preferred_element_type=jnp.float32)
    wide = wide + jnp.dot(pick_ref[1], second_ref[bank_rows:], preferred_element_type=jnp.float32)
    queries = wide.astype(jnp.bfloat16)
    part = scale_refs[0].shape[1]
    block = block_ref[...]
    picked = jnp.zeros(listed_ref.shape, jnp.float32)
    for c, (turned, scale) in enumerate(chunks(turned_refs, scale_refs)):
        scores = jnp.dot(queries, turned, preferred_element_type=jnp.float32) * scale
        for b in range(part // BLOCK):
            picked = jnp.where(block == c * (part // BLOCK) + b, scores[:, b * BLOCK : (b + 1) * BLOCK], picked)
    listed_ref[...] = jnp.exp2(picked * scales(wide))


def score_tests(order, bank_rows, first, second, turned, scale, slabs, offsets, colsum):
    slots = len(order) * CAP
    group = slabs.shape[1]
    return pl.pallas_call(
        functools.partial(test_kernel, order, bank_rows),
        out_shape=(
            pltpu.VMEM((slots, BLOCK), jnp.float32),
            pltpu.VMEM((slots, LANES), jnp.int32),
            pltpu.VMEM((group // len(order), slots), jnp.float32),
            pltpu.VMEM(colsum.shape, jnp.float32),
        ),
        in_specs=[VMEM] * (5 + 2 * len(PARTS)),
        out_specs=(VMEM,) * 4,
        scratch_shapes=[pltpu.VMEM((2, slots, group // 2), jnp.bfloat16)],
        compiler_params=PARAMS,
        name="score_tests",
    )(*map(keep, (first, second, *turned, *scale, slabs, offsets, colsum)))


def pool_kernel(order, listed_ref, own_ref, other_ref, block_ref, *refs):
    *gallery_refs, out_ref, weight_ref = refs
    block = block_ref[...]
    slots, rows = weight_ref.shape
    depth = gallery_refs[0].shape[1]
    each = rows // BLOCK // CHUNKS
    inverse = 1.0 / (own_ref[...] + other_ref[...])
    picked = jnp.zeros((slots, BLOCK), jnp.float32)
    for b in range(rows // BLOCK):
        c, at = b // each, (b % each) * BLOCK
        picked = jnp.where(block == b, inverse[c : c + 1, at : at + BLOCK], picked)
    weight = listed_ref[...] * picked
    total = jnp.sum(weight, axis=1, keepdims=True)
    for b in range(rows // BLOCK):
        weight_ref[:, b * BLOCK : (b + 1) * BLOCK] = jnp.where(block == b, weight, 0.0).astype(jnp.bfloat16)
    numerator, row = jnp.zeros((slots, depth), jnp.float32), 0
    for gallery_ref in gallery_refs:
        here = slice(row, row + gallery_ref.shape[0])
        numerator = numerator + jnp.dot(weight_ref[:, here], gallery_ref[...], preferred_element_type=jnp.float32)
        row = here.stop
    high = total.astype(jnp.bfloat16).astype(jnp.float32)
    lane = iota((slots, LANES), 1)
    tail = jnp.where(lane == 0, high, jnp.where(lane == 1, total - high, 0.0))
    me = lax.axis_index("gal")
    for i, bits in enumerate(order):
        at = slice(i * CAP, (i + 1) * CAP)
        out_ref[me ^ bits, :, :depth] = numerator[at].astype(jnp.bfloat16)
        out_ref[me ^ bits, :, depth:] = tail[at].astype(jnp.bfloat16)


def pool(order, listed, own, other, gallery, block):
    depth = gallery[0].shape[1]
    rows = sum(part.shape[0] for part in gallery)
    slots = listed.shape[0]
    return pl.pallas_call(
        functools.partial(pool_kernel, order),
        out_shape=pltpu.VMEM((len(order), CAP, depth + LANES), jnp.bfloat16),
        in_specs=[VMEM] * (4 + len(gallery)),
        out_specs=VMEM,
        scratch_shapes=[pltpu.VMEM((slots, rows), jnp.bfloat16)],
        compiler_params=PARAMS,
        name="pool",
    )(keep(listed), keep(own), other, keep(block), *map(keep, gallery))


def finish_kernel(sums_ref, spread_ref, out_ref):
    depth = out_ref.shape[1]
    sums = sums_ref[...].reshape(sums_ref.shape[0] * CAP, sums_ref.shape[2])
    sums = jnp.dot(spread_ref[...].astype(jnp.bfloat16), sums, preferred_element_type=jnp.float32)
    out_ref[...] = sums[:, :depth] / (sums[:, depth : depth + 1] + sums[:, depth + 1 : depth + 2])


def finish(sums, spread):
    return pl.pallas_call(
        finish_kernel,
        out_shape=jax.ShapeDtypeStruct((spread.shape[0], sums.shape[2] - LANES), jnp.float32),
        in_specs=[VMEM, VMEM],
        out_specs=VMEM,
        compiler_params=PARAMS,
        name="finish",
    )(sums, keep(spread))


def join_kernel(bank_own, own, *refs):
    *pieces, out_ref = refs
    bank, test = 0, sum(piece.shape[0] for piece in pieces) // own * bank_own
    for piece in pieces:
        rows = piece.shape[0]
        split = rows // own * bank_own
        out_ref[bank : bank + split, :] = piece[:split]
        out_ref[test : test + rows - split, :] = piece[split:]
        bank, test = bank + split, test + rows - split


def join(bank_own, test_own, pieces):
    rows = sum(piece.shape[0] for piece in pieces)
    return pl.pallas_call(
        functools.partial(join_kernel, bank_own, bank_own + test_own),
        out_shape=pltpu.VMEM((rows, pieces[0].shape[1]), pieces[0].dtype),
        in_specs=[VMEM] * len(pieces),
        out_specs=VMEM,
        compiler_params=PARAMS,
        name="join",
    )(*pieces)


def join_first(pieces):
    def kernel(*refs):
        *ins, out_ref = refs
        row = 0
        for piece in ins:
            out_ref[row : row + piece.shape[0], :] = piece[...]
            row += piece.shape[0]

    rows = sum(piece.shape[0] for piece in pieces)
    return pl.pallas_call(
        kernel,
        out_shape=pltpu.VMEM((rows, pieces[0].shape[1]), pieces[0].dtype),
        in_specs=[VMEM] * len(pieces),
        out_specs=VMEM,
        compiler_params=PARAMS,
        name="join",
    )(*pieces)


def swap(value, axis, size, bit):
    return lax.ppermute(value, axis, [(i, i ^ bit) for i in range(size)])


def body(devices, banks, bank_queries, gallery, test_queries, test_slabs, test_offsets):
    bank_own, test_own = bank_queries.shape[0], test_queries.shape[0]

    rounds = [[1 << k | 1] for k in range(devices.bit_length() - 2, 2, -1)] + [[3, 7, 4], [1]]
    order = [0]
    for masks in rounds:
        order = order + [o ^ mask for mask in masks for o in order]

    others = [swap(rows, "gal", devices, rounds[0][0]) for rows in (bank_queries, test_queries)]
    low, low_turned, low_scale, bank, test, slabs, offsets = load_low(
        gallery, bank_queries, test_queries, test_slabs.T, test_offsets.T
    )
    packed = join_first([bank, others[0], test, others[1]])
    for i, near in enumerate(rounds[1:]):
        if i:
            packed = join(bank_own, test_own, [packed, *others])
        others = [swap(packed, "gal", devices, mask) for mask in near]
        if i == 0:
            more, more_turned, more_scale, packed = load_more(gallery, packed)
        if i == len(rounds) - 2:
            last_turned, last_scale, packed = turn_last(gallery, more, packed)
    other = others[0]
    turned, scale = (low_turned, more_turned, last_turned), (low_scale, more_scale, last_scale)
    gallery = (low, more)

    bank_rows = devices // 2 * bank_own
    first, second = packed, other
    colsum = score_bank(bank_rows, first, second, turned, scale)
    bit = banks // 2
    other = jnp.zeros_like(colsum)
    while bit:
        other = swap(colsum, "bank", banks, bit)
        bit //= 2
        if bit:
            colsum = colsum + other
    listed, block, spread, colsum = score_tests(
        order, bank_rows, first, second, turned, scale, slabs, offsets, colsum
    )
    sums = pool(order, listed, colsum, other, gallery, block)
    sums = lax.all_to_all(sums, "gal", 0, 0, tiled=True)
    return finish(sums, spread)


def solution(mesh):
    in_specs = (
        P(("bank", "gal"), None),
        P("gal", None),
        P(("bank", "gal"), None),
        P("bank", None),
        P("bank", None),
    )
    out_specs = P(("bank", "gal"), None)
    local = functools.partial(body, mesh.shape["gal"], mesh.shape["bank"])
    return jax.shard_map(local, mesh=mesh, in_specs=in_specs, out_specs=out_specs, check_vma=False)
```

```python
import functools

import jax
import jax.numpy as jnp
from jax import lax
from jax.experimental import pallas as pl
from jax.experimental.pallas import tpu as pltpu
from jax.sharding import PartitionSpec as P

BLOCK = 128
CHUNKS = 8
PARTS = (4, 3, 1)
LANES = 128
CAP = 2
SHARPNESS = 20.0
LOG2E = 1.4426950408889634
epsilon = 1e-06

VMEM = pl.BlockSpec(memory_space=pltpu.VMEM)
HBM = pl.BlockSpec(memory_space=pltpu.HBM)
PARAMS = pltpu.CompilerParams(vmem_limit_bytes=16 << 20)


def in_hbm(value):
    return pltpu.with_memory_space_constraint(value, pltpu.HBM)


def keep(value):
    return pltpu.with_memory_space_constraint(value, pltpu.VMEM)


def bits_of(index, order):
    value = jnp.zeros_like(index)
    for place, mask in enumerate(order):
        value = jnp.where(index == place, mask, value)
    return value


def iota(shape, axis):
    return lax.broadcasted_iota(jnp.int32, shape, axis)


def route(order, test_own, slabs, offsets, pick_ref, block_ref, spread_ref):
    me = lax.axis_index("gal")
    devices = len(order)
    group = devices * test_own
    slots = devices * CAP

    found = jnp.sum(jnp.where(slabs == me, offsets + 1, 0), axis=0, keepdims=True)
    before = (iota((group, group), 0) // test_own == iota((group, group), 1) // test_own) & (
        iota((group, group), 0) < iota((group, group), 1)
    )
    flags = jnp.broadcast_to(jnp.where(found > 0, 1.0, 0.0), (8, group)).astype(jnp.bfloat16)
    rank = jnp.dot(flags, jnp.where(before, 1.0, 0.0).astype(jnp.bfloat16), preferred_element_type=jnp.float32)
    rank = rank[:1].astype(jnp.int32)
    index = iota((slots, group), 0)
    column = iota((slots, group), 1)
    filled = (column // test_own == me ^ bits_of(index // CAP, order)) & (found > 0) & (rank == index % CAP)
    block = jnp.sum(jnp.where(filled, found, 0), axis=1, keepdims=True) - 1
    block_ref[...] = jnp.broadcast_to(block, block_ref.shape)
    from_row = jnp.sum(jnp.where(filled, column % test_own + 1, 0), axis=1, keepdims=True)
    index = iota((slots, 1), 0) // CAP
    slot_from = jnp.where(from_row > 0, index * test_own - 1 + from_row, -1)
    half = pick_ref.shape[2]
    for h in range(2):
        column = iota((slots, half), 1) + h * half
        pick_ref[h] = jnp.where(column == slot_from, 1.0, 0.0).astype(jnp.bfloat16)

    lane = iota((1, slots), 1)
    filled_before = jnp.zeros((1, slots), jnp.int32)
    mine = iota(slabs.shape, 1)
    for r in range(test_own):
        listed = jnp.sum(jnp.where(mine == me * test_own + r, slabs, 0), axis=1, keepdims=True)
        here = jnp.sum(jnp.where(listed == lane // CAP, 1, 0), axis=0, keepdims=True)
        spread_ref[r : r + 1, :] = jnp.where((here > 0) & (filled_before == lane % CAP), 1.0, 0.0)
        filled_before = filled_before + here


def fetch(gallery_hbm, first_row, gallery_ref, sems):
    part = gallery_hbm.shape[0] // CHUNKS
    copies = [
        pltpu.make_async_copy(
            gallery_hbm.at[pl.ds(first_row + c * part, part)], gallery_ref.at[pl.ds(c * part, part)], sems.at[c]
        )
        for c in range(gallery_ref.shape[0] // part)
    ]
    for copy in copies:
        copy.start()
    return copies


def turn(c, at, gallery_ref, turned_ref, scale_ref):
    part = scale_ref.shape[1]
    turned = gallery_ref[pl.ds(at * part, part), :].T
    turned_ref[:, c * part : (c + 1) * part] = turned
    values = turned.astype(jnp.float32)
    scale_ref[c : c + 1, :] = lax.rsqrt(jnp.sum(values * values, axis=0, keepdims=True) + epsilon)


def low_kernel(
    gallery_hbm, bank_hbm, test_hbm, slabs_hbm, offsets_hbm,
    gallery_ref, turned_ref, scale_ref, bank_ref, test_ref, slabs_ref, offsets_ref, sems, small_sems,
):
    pairs = ((bank_hbm, bank_ref), (test_hbm, test_ref), (slabs_hbm, slabs_ref), (offsets_hbm, offsets_ref))
    small = [pltpu.make_async_copy(*pair, small_sems.at[i]) for i, pair in enumerate(pairs)]
    copies = fetch(gallery_hbm, 0, gallery_ref, sems)
    for copy in small:
        copy.start()
    for c, copy in enumerate(copies):
        copy.wait()
        turn(c, c, gallery_ref, turned_ref, scale_ref)
    for copy in small:
        copy.wait()


def more_kernel(gallery_hbm, packed_ref, gallery_ref, turned_ref, scale_ref, packed_out, sems):
    copies = fetch(gallery_hbm, gallery_hbm.shape[0] - gallery_ref.shape[0], gallery_ref, sems)
    packed_out[...] = packed_ref[...]
    for c, copy in enumerate(copies):
        copy.wait()
        if c < scale_ref.shape[0]:
            turn(c, c, gallery_ref, turned_ref, scale_ref)


def last_kernel(gallery_ref, packed_ref, turned_ref, scale_ref, packed_out):
    packed_out[...] = packed_ref[...]
    for c in range(scale_ref.shape[0]):
        turn(c, PARTS[1] + c, gallery_ref, turned_ref, scale_ref)


def part_shapes(gallery, parts):
    rows, depth = gallery.shape
    part = rows // CHUNKS
    return (
        pltpu.VMEM((depth, parts * part), gallery.dtype),
        pltpu.VMEM((parts, part), jnp.float32),
    )


def rows_shape(gallery, parts):
    rows, depth = gallery.shape
    return pltpu.VMEM((rows // CHUNKS * parts, depth), gallery.dtype)


def load_low(gallery, *small):
    return pl.pallas_call(
        low_kernel,
        out_shape=(rows_shape(gallery, PARTS[0]), *part_shapes(gallery, PARTS[0]), *(pltpu.VMEM(x.shape, x.dtype) for x in small)),
        in_specs=[HBM] * 5,
        out_specs=(VMEM,) * 7,
        scratch_shapes=[pltpu.SemaphoreType.DMA((PARTS[0],)), pltpu.SemaphoreType.DMA((4,))],
        compiler_params=PARAMS,
        name="load_low",
    )(*map(in_hbm, (gallery, *small)))


def load_more(gallery, packed):
    parts = CHUNKS - PARTS[0]
    return pl.pallas_call(
        more_kernel,
        out_shape=(
            rows_shape(gallery, parts),
            *part_shapes(gallery, PARTS[1]),
            pltpu.VMEM(packed.shape, packed.dtype),
        ),
        in_specs=[HBM, VMEM],
        out_specs=(VMEM,) * 4,
        scratch_shapes=[pltpu.SemaphoreType.DMA((parts,))],
        compiler_params=PARAMS,
        name="load_more",
    )(in_hbm(gallery), packed)


def turn_last(gallery, more, packed):
    return pl.pallas_call(
        last_kernel,
        out_shape=(*part_shapes(gallery, PARTS[2]), pltpu.VMEM(packed.shape, packed.dtype)),
        in_specs=[VMEM, VMEM],
        out_specs=(VMEM,) * 3,
        compiler_params=PARAMS,
        name="turn_last",
    )(keep(more), packed)


def scales(wide):
    return lax.rsqrt(jnp.sum(wide * wide, axis=1, keepdims=True) + epsilon) * (SHARPNESS * LOG2E)


def chunks(turned_refs, scale_refs):
    for turned_ref, scale_ref in zip(turned_refs, scale_refs):
        parts, part = scale_ref.shape
        for c in range(parts):
            yield turned_ref[:, c * part : (c + 1) * part], scale_ref[c : c + 1, :]


def bank_kernel(bank_rows, first_ref, second_ref, *refs):
    number = len(PARTS)
    turned_refs, scale_refs, colsum_ref = refs[:number], refs[number : 2 * number], refs[-1]
    queries = jnp.concatenate([first_ref[:bank_rows], second_ref[:bank_rows]], axis=0)
    query_scale = scales(queries.astype(jnp.float32))
    for c, (turned, scale) in enumerate(chunks(turned_refs, scale_refs)):
        scores = jnp.dot(queries, turned, preferred_element_type=jnp.float32)
        exps = jnp.exp2(scores * scale * query_scale)
        colsum_ref[c : c + 1, :] = jnp.sum(exps, axis=0, keepdims=True)


def score_bank(bank_rows, first, second, turned, scale):
    return pl.pallas_call(
        functools.partial(bank_kernel, bank_rows),
        out_shape=pltpu.VMEM((CHUNKS, scale[0].shape[1]), jnp.float32),
        in_specs=[VMEM] * (2 + 2 * len(PARTS)),
        out_specs=VMEM,
        compiler_params=PARAMS,
        name="score_bank",
    )(keep(first), second, *map(keep, turned), *map(keep, scale))


def test_kernel(order, bank_rows, first_ref, second_ref, *refs):
    number = len(PARTS)
    turned_refs, scale_refs, refs = refs[:number], refs[number : 2 * number], refs[2 * number :]
    slabs_ref, offsets_ref, colsum_ref, listed_ref, block_ref, spread_ref, colsum_out, pick_ref = refs
    colsum_out[...] = colsum_ref[...]
    route(order, spread_ref.shape[0], slabs_ref[...], offsets_ref[...], pick_ref, block_ref, spread_ref)
    wide = jnp.dot(pick_ref[0], first_ref[bank_rows:], preferred_element_type=jnp.float32)
    wide = wide + jnp.dot(pick_ref[1], second_ref[bank_rows:], preferred_element_type=jnp.float32)
    queries = wide.astype(jnp.bfloat16)
    part = scale_refs[0].shape[1]
    block = block_ref[...]
    picked = jnp.zeros(listed_ref.shape, jnp.float32)
    for c, (turned, scale) in enumerate(chunks(turned_refs, scale_refs)):
        scores = jnp.dot(queries, turned, preferred_element_type=jnp.float32) * scale
        for b in range(part // BLOCK):
            picked = jnp.where(block == c * (part // BLOCK) + b, scores[:, b * BLOCK : (b + 1) * BLOCK], picked)
    listed_ref[...] = jnp.exp2(picked * scales(wide))


def score_tests(order, bank_rows, first, second, turned, scale, slabs, offsets, colsum):
    slots = len(order) * CAP
    group = slabs.shape[1]
    return pl.pallas_call(
        functools.partial(test_kernel, order, bank_rows),
        out_shape=(
            pltpu.VMEM((slots, BLOCK), jnp.float32),
            pltpu.VMEM((slots, LANES), jnp.int32),
            pltpu.VMEM((group // len(order), slots), jnp.float32),
            pltpu.VMEM(colsum.shape, jnp.float32),
        ),
        in_specs=[VMEM] * (5 + 2 * len(PARTS)),
        out_specs=(VMEM,) * 4,
        scratch_shapes=[pltpu.VMEM((2, slots, group // 2), jnp.bfloat16)],
        compiler_params=PARAMS,
        name="score_tests",
    )(*map(keep, (first, second, *turned, *scale, slabs, offsets, colsum)))


def pool_kernel(order, listed_ref, own_ref, other_ref, block_ref, *refs):
    *gallery_refs, out_ref, weight_ref = refs
    block = block_ref[...]
    slots, rows = weight_ref.shape
    depth = gallery_refs[0].shape[1]
    each = rows // BLOCK // CHUNKS
    inverse = 1.0 / (own_ref[...] + other_ref[...])
    picked = jnp.zeros((slots, BLOCK), jnp.float32)
    for b in range(rows // BLOCK):
        c, at = b // each, (b % each) * BLOCK
        picked = jnp.where(block == b, inverse[c : c + 1, at : at + BLOCK], picked)
    weight = listed_ref[...] * picked
    total = jnp.sum(weight, axis=1, keepdims=True)
    for b in range(rows // BLOCK):
        weight_ref[:, b * BLOCK : (b + 1) * BLOCK] = jnp.where(block == b, weight, 0.0).astype(jnp.bfloat16)
    numerator, row = jnp.zeros((slots, depth), jnp.float32), 0
    for gallery_ref in gallery_refs:
        here = slice(row, row + gallery_ref.shape[0])
        numerator = numerator + jnp.dot(weight_ref[:, here], gallery_ref[...], preferred_element_type=jnp.float32)
        row = here.stop
    high = total.astype(jnp.bfloat16).astype(jnp.float32)
    lane = iota((slots, LANES), 1)
    tail = jnp.where(lane == 0, high, jnp.where(lane == 1, total - high, 0.0))
    me = lax.axis_index("gal")
    for i, bits in enumerate(order):
        at = slice(i * CAP, (i + 1) * CAP)
        out_ref[me ^ bits, :, :depth] = numerator[at].astype(jnp.bfloat16)
        out_ref[me ^ bits, :, depth:] = tail[at].astype(jnp.bfloat16)


def pool(order, listed, own, other, gallery, block):
    depth = gallery[0].shape[1]
    rows = sum(part.shape[0] for part in gallery)
    slots = listed.shape[0]
    return pl.pallas_call(
        functools.partial(pool_kernel, order),
        out_shape=pltpu.VMEM((len(order), CAP, depth + LANES), jnp.bfloat16),
        in_specs=[VMEM] * (4 + len(gallery)),
        out_specs=VMEM,
        scratch_shapes=[pltpu.VMEM((slots, rows), jnp.bfloat16)],
        compiler_params=PARAMS,
        name="pool",
    )(keep(listed), keep(own), other, keep(block), *map(keep, gallery))


def finish_kernel(sums_ref, spread_ref, out_ref):
    depth = out_ref.shape[1]
    sums = sums_ref[...].reshape(sums_ref.shape[0] * CAP, sums_ref.shape[2])
    sums = jnp.dot(spread_ref[...].astype(jnp.bfloat16), sums, preferred_element_type=jnp.float32)
    out_ref[...] = sums[:, :depth] / (sums[:, depth : depth + 1] + sums[:, depth + 1 : depth + 2])


def finish(sums, spread):
    return pl.pallas_call(
        finish_kernel,
        out_shape=jax.ShapeDtypeStruct((spread.shape[0], sums.shape[2] - LANES), jnp.float32),
        in_specs=[VMEM, VMEM],
        out_specs=VMEM,
        compiler_params=PARAMS,
        name="finish",
    )(sums, keep(spread))


def join_kernel(bank_own, own, *refs):
    *pieces, out_ref = refs
    bank, test = 0, sum(piece.shape[0] for piece in pieces) // own * bank_own
    for piece in pieces:
        rows = piece.shape[0]
        split = rows // own * bank_own
        out_ref[bank : bank + split, :] = piece[:split]
        out_ref[test : test + rows - split, :] = piece[split:]
        bank, test = bank + split, test + rows - split


def join(bank_own, test_own, pieces):
    rows = sum(piece.shape[0] for piece in pieces)
    return pl.pallas_call(
        functools.partial(join_kernel, bank_own, bank_own + test_own),
        out_shape=pltpu.VMEM((rows, pieces[0].shape[1]), pieces[0].dtype),
        in_specs=[VMEM] * len(pieces),
        out_specs=VMEM,
        compiler_params=PARAMS,
        name="join",
    )(*pieces)


def join_first(pieces):
    def kernel(*refs):
        *ins, out_ref = refs
        row = 0
        for piece in ins:
            out_ref[row : row + piece.shape[0], :] = piece[...]
            row += piece.shape[0]

    rows = sum(piece.shape[0] for piece in pieces)
    return pl.pallas_call(
        kernel,
        out_shape=pltpu.VMEM((rows, pieces[0].shape[1]), pieces[0].dtype),
        in_specs=[VMEM] * len(pieces),
        out_specs=VMEM,
        compiler_params=PARAMS,
        name="join",
    )(*pieces)


def swap(value, axis, size, bit):
    return lax.ppermute(value, axis, [(i, i ^ bit) for i in range(size)])


def body(devices, banks, bank_queries, gallery, test_queries, test_slabs, test_offsets):
    bank_own, test_own = bank_queries.shape[0], test_queries.shape[0]

    rounds = [[1 << k | 1] for k in range(devices.bit_length() - 2, 2, -1)] + [[3, 7, 4], [1]]
    order = [0]
    for masks in rounds:
        order = order + [o ^ mask for mask in masks for o in order]

    others = [swap(rows, "gal", devices, rounds[0][0]) for rows in (bank_queries, test_queries)]
    low, low_turned, low_scale, bank, test, slabs, offsets = load_low(
        gallery, bank_queries, test_queries, test_slabs.T, test_offsets.T
    )
    packed = join_first([bank, others[0], test, others[1]])
    for i, near in enumerate(rounds[1:]):
        if i:
            packed = join(bank_own, test_own, [packed, *others])
        others = [swap(packed, "gal", devices, mask) for mask in near]
        if i == 0:
            more, more_turned, more_scale, packed = load_more(gallery, packed)
        if i == len(rounds) - 2:
            last_turned, last_scale, packed = turn_last(gallery, more, packed)
    other = others[0]
    turned, scale = (low_turned, more_turned, last_turned), (low_scale, more_scale, last_scale)
    gallery = (low, more)

    bank_rows = devices // 2 * bank_own
    first, second = packed, other
    colsum = score_bank(bank_rows, first, second, turned, scale)
    bit = banks // 2
    other = jnp.zeros_like(colsum)
    while bit:
        other = swap(colsum, "bank", banks, bit)
        bit //= 2
        if bit:
            colsum = colsum + other
    listed, block, spread, colsum = score_tests(
        order, bank_rows, first, second, turned, scale, slabs, offsets, colsum
    )
    sums = pool(order, listed, colsum, other, gallery, block)
    sums = lax.all_to_all(sums, "gal", 0, 0, tiled=True)
    return finish(sums, spread)


def solution(mesh):
    in_specs = (
        P(("bank", "gal"), None),
        P("gal", None),
        P(("bank", "gal"), None),
        P("bank", None),
        P("bank", None),
    )
    out_specs = P(("bank", "gal"), None)
    local = functools.partial(body, mesh.shape["gal"], mesh.shape["bank"])
    return jax.shard_map(local, mesh=mesh, in_specs=in_specs, out_specs=out_specs, check_vma=False)
```
